512 devices in a mesh: dp: 128 (over y, z_hi, x), mp: 4 (over z_lo, core).
Axes of the slice: x: 4, y: 8, z: 8 (z_hi: 4, z_lo: 2; z = z_hi * 2 + z_lo), core: 2. Of those that a mesh axis runs over, the one named last changes fastest.
Arguments:
- frames: bfloat16 [2048, 32, 1408], P('dp', None, 'mp'), may hold values from -6 to 6
- frame_counts: int32 [2048], P('dp'), may hold values from 1 to 32, 32768 in all
- norm_gain: float32 [1408], replicated, may hold values from 0.5 to 1.5
- norm_bias: float32 [1408], replicated, may hold values from -3 to 3
- up_weight: bfloat16 [1408, 3072], P('dp', 'mp'), may hold values from -0.15625 to 0.15625
- up_bias: float32 [3072], P('mp'), may hold values from -3 to 3
- down_weight: bfloat16 [1408, 3072], P('dp', 'mp'), may hold values from -0.109375 to 0.109375
- down_bias: float32 [1408], replicated, may hold values from -3 to 3
- final_gain: float32 [1408], P('mp'), may hold values from 0.5 to 1.5
- final_bias: float32 [1408], P('mp'), may hold values from -3 to 3
- projection: bfloat16 [1408, 1024], P('mp'), may hold values from -0.15625 to 0.15625
- captions: bfloat16 [2048, 1024], P(('dp', 'mp')), may hold values from -6 to 6
- positives: int32 [2048], P('dp'), may hold values from 0 to 2047, each once
- logit_scale: float32 [], replicated, may hold values from 8 to 16
- logit_bias: float32 [], replicated, may hold values from -5 to -2
Outputs:
- video_embed: float32 [2048, 1024], P('dp')
- video_grad: float32 [2048, 1024], P('dp')
- text_grad: float32 [2048, 1024], P(('dp', 'mp'))
The draws below stay inside these ranges and needn't reach their ends.
Inputs may be any that keep to these rules, and one draw needn't show every extreme that they name: `frame_counts`: the counts sum to 32768, and some clip has 32 frames. `positives`: every caption is the match of exactly one clip.
All inputs are finite; a program needn't handle non-finite values. No bound on the sum of `frame_counts` on one device may be relied on, other than what follows from the above.
Results may differ from the reference program's by a relative error of at most 0.015.
Values may be sent and summed in bfloat16 or wider, within the bound.
A program may use at most 64 MiB of HBM per device.

```python
import math
import jax
import jax.numpy as jnp
import numpy as np
from jax import lax

D = 1408
FF = 3072
E = 1024
MAXF = 32
CLIPS = 2048
N_MP = 4


def draw_frames(key, part):
    key = jax.random.fold_in(key, 11)
    content_key = jax.random.fold_in(key, 1)
    frame_key = jax.random.fold_in(key, 2)
    clip_content = jax.random.normal(content_key, (CLIPS, 1, D), jnp.float32)
    frame_noise = 0.5 * jax.random.normal(frame_key, (CLIPS, MAXF, D), jnp.float32)
    return jnp.clip(clip_content + frame_noise, -6.0, 6.0).astype(jnp.bfloat16)


def steps_of(rng, dims, cuts, low, largest):
    factor_of = 1.0
    for dim, shards_of in cuts:
        steps = jax.random.uniform(jax.random.fold_in(jax.random.fold_in(rng, 6), dim), (shards_of,), jnp.float32, low / len(cuts), largest / len(cuts))
        factor_of = factor_of * jnp.repeat(jnp.exp(steps), dims[dim] // shards_of).reshape((-1,) + (1,) * (len(dims) - 1 - dim))
    return factor_of


def profile(count, total, limit, slope):
    portions = [(1 << 20) // math.isqrt(rank ** slope) + 1 for rank in range(2, count + 1)]
    surplus, holding = total - limit - (count - 1), [1] * (count - 1)
    while surplus > 0:
        candidates = [i for i in range(count - 1) if holding[i] < limit]
        pool, left = sum([portions[i] for i in candidates]), surplus
        for i in candidates:
            extra = min(limit - holding[i], max(1, left * portions[i] // pool), surplus)
            holding[i] = holding[i] + extra
            surplus = surplus - extra
    return np.array([limit] + holding)


def ragged(rng, count, total, most, lean):
    if count == 2:
        one = jax.random.randint(rng, (), max(1, total - most), min(most, total - 1) + 1)
        return jnp.stack([one, total - one])
    tallies = jnp.asarray(profile(count, total, most, lean), jnp.int32)
    twos = (count - 1) // 2
    donor, taker = tallies[1:1 + 2 * twos:2], tallies[2:2 + 2 * twos:2]
    room = jnp.minimum(donor - 1, most - taker)
    moved = jax.random.randint(jax.random.fold_in(rng, 1), (twos,), 0, 1 << 20) % (room + 1)
    tallies = tallies.at[1:1 + 2 * twos:2].set(donor - moved).at[2:2 + 2 * twos:2].set(taker + moved)
    return tallies[jax.random.permutation(jax.random.fold_in(rng, 2), count)]


def gaussian(stream_key, shape, deviation, limit, split=(), kind=jnp.bfloat16):
    drawn = jax.random.normal(stream_key, shape, jnp.float32) * deviation
    if len(split) > 0:
        drawn = steps_of(stream_key, shape, split, -0.22, 0.18) * drawn
    return jnp.clip(drawn, min=-limit, max=limit).astype(kind)


def setup_inputs(seed: int = 0) -> dict:
    seeds = jax.random.split(jax.random.key(seed), 16)
    frames = draw_frames(jax.random.fold_in(seeds[15], 71), 0)
    frame_counts = ragged(seeds[1], CLIPS, CLIPS * MAXF // 2, MAXF, 2).astype(jnp.int32)
    norm_gain = jnp.clip(1.0 + 0.1 * jax.random.normal(seeds[2], (D,), jnp.float32), 0.5, 1.5)
    norm_bias = gaussian(seeds[3], (D,), 0.2, 3.0, (), jnp.float32)
    up_weight = gaussian(seeds[4], (D, FF), D ** -0.5, 0.15625, ((0, 128), (1, 4)))
    up_bias = gaussian(seeds[5], (FF,), 0.2, 3.0, ((0, 4),), jnp.float32)
    down_weight = gaussian(seeds[6], (D, FF), FF ** -0.5, 0.109375, ((0, 128), (1, 4)))
    down_bias = gaussian(seeds[7], (D,), 0.2, 3.0, (), jnp.float32)
    final_gain = jnp.clip(1.0 + 0.1 * jax.random.normal(seeds[8], (D,), jnp.float32), 0.5, 1.5)
    final_bias = gaussian(seeds[9], (D,), 0.2, 3.0, ((0, 4),), jnp.float32)
    projection = gaussian(seeds[10], (D, E), D ** -0.5, 0.15625, ((0, 4),))
    captions = gaussian(seeds[11], (CLIPS, E), 1.0, 6.0, ((0, 512),))
    positives = jax.random.permutation(seeds[12], CLIPS).astype(jnp.int32)
    logit_scale = jnp.clip(jnp.exp(jax.random.uniform(seeds[13], (), jnp.float32, math.log(8.0), math.log(16.0))), 8.0, 16.0)
    logit_bias = jnp.clip(jax.random.uniform(seeds[14], (), jnp.float32, -5.0, -2.0), -5.0, -2.0)
    return {"frames": frames, "frame_counts": frame_counts, "norm_gain": norm_gain, "norm_bias": norm_bias, "up_weight": up_weight, "up_bias": up_bias, "down_weight": down_weight, "down_bias": down_bias, "final_gain": final_gain, "final_bias": final_bias, "projection": projection, "captions": captions, "positives": positives, "logit_scale": logit_scale, "logit_bias": logit_bias}


epsilon = 1e-06

def normalise_moments(values, gain, shift):
    row_mean = lax.optimization_barrier(jnp.mean(values, axis=-1, keepdims=True))
    square_mean = lax.optimization_barrier(jnp.mean(values * values, axis=-1, keepdims=True))
    variance = square_mean - row_mean * row_mean
    return (values - row_mean) * lax.rsqrt(variance + epsilon) * gain + shift

def reference(frames, frame_counts, norm_gain, norm_bias, up_weight, up_bias, down_weight, down_bias, final_gain, final_bias, projection, captions, positives, logit_scale, logit_bias):
    frame_rows = frames.reshape(CLIPS * MAXF, D).astype(jnp.float32)
    normed = normalise_moments(frame_rows, norm_gain, norm_bias).astype(jnp.bfloat16)
    quarter = FF // N_MP
    branch = jnp.zeros((CLIPS * MAXF, D), jnp.float32)
    for slot in range(N_MP):
        low = slot * quarter
        up_sum = jnp.dot(normed, up_weight[:, low:low + quarter], preferred_element_type=jnp.float32) + up_bias[low:low + quarter]
        hidden = jax.nn.gelu(up_sum, approximate=False).astype(jnp.bfloat16)
        partial_value = lax.dot_general(hidden, down_weight[:, low:low + quarter], (((1,), (1,)), ((), ())), preferred_element_type=jnp.float32)
        rounded = lax.optimization_barrier(partial_value.astype(jnp.bfloat16))
        branch = branch + rounded.astype(jnp.float32)
    resid = frame_rows + branch + down_bias
    final_rows = normalise_moments(resid, final_gain, final_bias).reshape(CLIPS, MAXF, D)
    frame_mask = (jnp.arange(MAXF, dtype=jnp.int32)[None, :] < frame_counts[:, None]).astype(jnp.float32)
    pooled = lax.optimization_barrier(jnp.sum(final_rows * frame_mask[:, :, None], axis=1)) / frame_counts[:, None].astype(jnp.float32)
    pooled = pooled.astype(jnp.bfloat16)
    raw = jnp.dot(pooled, projection, preferred_element_type=jnp.float32)
    video_embed = raw * lax.rsqrt(lax.optimization_barrier(jnp.sum(raw * raw, axis=-1, keepdims=True)) + epsilon)
    video_unit = video_embed.astype(jnp.bfloat16)
    caption_values = captions.astype(jnp.float32)
    text_unit = (caption_values * lax.rsqrt(lax.optimization_barrier(jnp.sum(caption_values * caption_values, axis=-1, keepdims=True)) + epsilon)).astype(jnp.bfloat16)
    logits = logit_scale * jnp.dot(video_unit, text_unit.T, preferred_element_type=jnp.float32) + logit_bias
    column_ids = jnp.arange(CLIPS, dtype=jnp.int32)
    labels = jnp.where(column_ids[None, :] == positives[:, None], jnp.float32(1.0), jnp.float32(-1.0))
    pair_weights = (-labels * jax.nn.sigmoid(-labels * logits)).astype(jnp.bfloat16)
    video_grad = logit_scale * jnp.dot(pair_weights, text_unit, preferred_element_type=jnp.float32)
    text_grad = logit_scale * jnp.dot(pair_weights.T, video_unit, preferred_element_type=jnp.float32)
    return (video_embed, video_grad, text_grad)
```

```python
import functools

import jax
import jax.numpy as jnp
from jax import lax
from jax.experimental import pallas as pl
from jax.experimental.pallas import tpu as pltpu
from jax.sharding import PartitionSpec as P

D = 1408
E = 1024
NY, NZ, NX, NM = 8, 4, 4, 4
MESH = pl.DeviceIdType.MESH
epsilon = 1e-06
F32 = jnp.float32
BF16 = jnp.bfloat16


def position():
    dp = lax.axis_index("dp")
    mp = lax.axis_index("mp")
    return dp // (NZ * NX), (dp // NX) % NZ, dp % NX, mp


def device(y, z, x, m):
    return ((y * NZ + z) * NX + x, m)


def peer_at(axis, step):
    y, z, x, m = position()
    if axis == "y":
        place = (y + step) % NY
        return device(place, z, x, m), place
    if axis == "z":
        place = (z + step) % NZ
        return device(y, place, x, m), place
    if axis == "x":
        place = (x + step) % NX
        return device(y, z, place, m), place
    place = (m + step) % NM
    return device(y, z, x, place), place


SIZES = {"y": NY, "z": NZ, "x": NX, "m": NM}


def greet():
    barrier = pltpu.get_barrier_semaphore()
    total = 0
    for axis, size in SIZES.items():
        for step in range(1, size):
            target, _ = peer_at(axis, step)
            pl.semaphore_signal(barrier, inc=1, device_id=target, device_id_type=MESH)
            total += 1
    pl.semaphore_wait(barrier, total)


class Exchange:
    def __init__(self, axis, source, slots, send_sem, recv_sem):
        self.axis, self.source, self.slots = axis, source, slots
        self.send_sem, self.recv_sem = send_sem, recv_sem
        y, z, x, m = position()
        self.own = {"y": y, "z": z, "x": x, "m": m}[axis]

    def copy(self, step):
        target, place = peer_at(self.axis, step)
        return pltpu.make_async_remote_copy(
            src_ref=self.source(place),
            dst_ref=self.slots.at[self.own],
            send_sem=self.send_sem.at[step],
            recv_sem=self.recv_sem.at[self.own],
            device_id=target,
            device_id_type=MESH,
        )

    def start(self):
        for step in range(1, SIZES[self.axis]):
            self.copy(step).start()

    def wait(self):
        for step in range(1, SIZES[self.axis]):
            target, place = peer_at(self.axis, step)
            pltpu.make_async_remote_copy(
                src_ref=self.source(place),
                dst_ref=self.slots.at[place],
                send_sem=self.send_sem.at[step],
                recv_sem=self.recv_sem.at[place],
                device_id=target,
                device_id_type=MESH,
            ).wait_recv()
        for step in range(1, SIZES[self.axis]):
            self.copy(step).wait_send()


def loss_kernel(
    raw_ref,
    captions_ref,
    positives_ref,
    scalars_ref,
    embed_ref,
    video_ref,
    text_ref,
    text_z,
    text_rows,
    text_y,
    video_x,
    where_x,
    text_out,
    text_in,
    video_out,
    video_in,
    text_sum,
    text_part,
    text_last,
    mp_in,
    send_sems,
    recv_sems,
):
    y, z, x, m = position()
    scale = scalars_ref[0]
    bias = scalars_ref[1]
    greet()
    caption_values = captions_ref[...].astype(F32)
    text_unit = caption_values * lax.rsqrt(
        jnp.sum(caption_values * caption_values, axis=-1, keepdims=True) + epsilon
    )
    text_z[z] = text_unit
    gather_text_z = Exchange("z", lambda place: text_z.at[z], text_z, send_sems.at[0], recv_sems.at[0])
    gather_text_z.start()
    where_x[x] = positives_ref[...]
    gather_where = Exchange("x", lambda place: where_x.at[x], where_x, send_sems.at[1], recv_sems.at[1])
    gather_where.start()
    raw = raw_ref[...]
    embed = raw * lax.rsqrt(jnp.sum(raw * raw, axis=-1, keepdims=True) + epsilon)
    embed_ref[...] = embed
    video_x[x] = embed.astype(BF16)
    gather_video = Exchange("x", lambda place: video_x.at[x], video_x, send_sems.at[2], recv_sems.at[2])
    gather_video.start()
    gather_text_z.wait()
    for slot in range(NZ):
        text_rows[4 * slot : 4 * slot + 4, :] = text_z[slot]
    text_y[y] = text_rows[...].astype(BF16)
    gather_text_y = Exchange("y", lambda place: text_y.at[y], text_y, send_sems.at[3], recv_sems.at[3])
    gather_text_y.start()
    gather_where.wait()
    gather_video.wait()
    gather_text_y.wait()

    text = text_y[...].reshape(NY * 16, E)
    video = video_x[...].reshape(NX * 16, E)
    logits = scale * lax.dot_general(
        video, text, (((1,), (1,)), ((), ())), preferred_element_type=F32
    ) + bias
    column = lax.broadcasted_iota(jnp.int32, (NX * 16, NY * 16), 1)
    owner = lax.shift_right_logical(column, 2)
    ids = (((owner * 4) + x) * 4 + m) * 4 + lax.bitwise_and(column, 3)
    labels = jnp.where(ids == where_x[...].reshape(NX * 16, 128), F32(1.0), F32(-1.0))
    pair_weights = -labels * lax.logistic(-labels * logits)
    turned = jnp.transpose(pair_weights).astype(BF16)
    text_terms = scale * jnp.dot(turned, video, preferred_element_type=F32)
    text_out[...] = text_terms.astype(BF16).reshape(NY, 16, E)
    text_in[y] = text_out[y]
    reduce_text_y = Exchange("y", lambda place: text_out.at[place], text_in, send_sems.at[4], recv_sems.at[4])
    reduce_text_y.start()
    video_terms = scale * jnp.dot(pair_weights.astype(BF16), text, preferred_element_type=F32)
    video_out[...] = video_terms.astype(BF16).reshape(NX, 16, E)
    video_in[x] = video_out[x]
    reduce_video_x = Exchange("x", lambda place: video_out.at[place], video_in, send_sems.at[5], recv_sems.at[5])
    reduce_video_x.start()

    reduce_video_x.wait()
    video_total = video_in[0].astype(F32)
    for slot in range(1, NX):
        video_total += video_in[slot].astype(F32)
    mp_in[m] = video_total.astype(BF16)
    share_video = Exchange("m", lambda place: mp_in.at[m], mp_in, send_sems.at[6], recv_sems.at[6])
    share_video.start()
    reduce_text_y.wait()
    text_total = text_in[0].astype(F32)
    for slot in range(1, NY):
        text_total += text_in[slot].astype(F32)
    text_sum[...] = text_total
    for slot in range(NZ):
        text_part[slot] = text_sum[4 * slot : 4 * slot + 4, :]
    text_last[z] = text_part[z]
    reduce_text_z = Exchange("z", lambda place: text_part.at[place], text_last, send_sems.at[7], recv_sems.at[7])
    reduce_text_z.start()
    share_video.wait()
    video_grad = mp_in[0].astype(F32)
    for slot in range(1, NM):
        video_grad += mp_in[slot].astype(F32)
    video_ref[...] = video_grad
    reduce_text_z.wait()
    text_grad = text_last[0]
    for slot in range(1, NZ):
        text_grad += text_last[slot]
    text_ref[...] = text_grad


def loss_part(raw, captions, positives, logit_scale, logit_bias):
    vmem = pl.BlockSpec(memory_space=pltpu.VMEM)
    return pl.pallas_call(
        loss_kernel,
        out_shape=(
            jax.ShapeDtypeStruct((16, E), F32),
            jax.ShapeDtypeStruct((16, E), F32),
            jax.ShapeDtypeStruct((4, E), F32),
        ),
        in_specs=[vmem, vmem, vmem, pl.BlockSpec(memory_space=pltpu.SMEM)],
        out_specs=(vmem, vmem, vmem),
        scratch_shapes=[
            pltpu.VMEM((NZ, 4, E), F32),
            pltpu.VMEM((16, E), F32),
            pltpu.VMEM((NY, 16, E), BF16),
            pltpu.VMEM((NX, 16, E), BF16),
            pltpu.VMEM((NX, 16, 128), jnp.int32),
            pltpu.VMEM((NY, 16, E), BF16),
            pltpu.VMEM((NY, 16, E), BF16),
            pltpu.VMEM((NX, 16, E), BF16),
            pltpu.VMEM((NX, 16, E), BF16),
            pltpu.VMEM((16, E), F32),
            pltpu.VMEM((NZ, 4, E), F32),
            pltpu.VMEM((NZ, 4, E), F32),
            pltpu.VMEM((NM, 16, E), BF16),
            pltpu.SemaphoreType.DMA((8, 8)),
            pltpu.SemaphoreType.DMA((8, 8)),
        ],
        compiler_params=pltpu.CompilerParams(
            collective_id=0, has_side_effects=True, vmem_limit_bytes=48 * 1024 * 1024
        ),
    )(
        raw,
        captions,
        jnp.broadcast_to(positives[:, None], (16, 128)),
        jnp.stack([logit_scale, logit_bias]),
    )


def on_device(
    frames,
    frame_counts,
    norm_gain,
    norm_bias,
    up_weight,
    up_bias,
    down_weight,
    down_bias,
    final_gain,
    final_bias,
    projection,
    captions,
    positives,
    logit_scale,
    logit_bias,
):
    clip_count, slot_count, local_width = frames.shape
    row_count = clip_count * slot_count
    gathered = lax.all_gather(frames, "mp", axis=2, tiled=True)
    frame_rows = gathered.reshape(row_count, D).astype(jnp.float32)
    row_mean = jnp.mean(frame_rows, axis=-1, keepdims=True)
    square_mean = jnp.mean(frame_rows * frame_rows, axis=-1, keepdims=True)
    normed = (
        (frame_rows - row_mean) * lax.rsqrt(square_mean - row_mean * row_mean + epsilon) * norm_gain
        + norm_bias
    ).astype(jnp.bfloat16)
    up_sum = jnp.dot(
        normed,
        lax.all_gather(up_weight, "dp", axis=0, tiled=True),
        preferred_element_type=jnp.float32,
    )
    hidden = jax.nn.gelu(up_sum + up_bias, approximate=False).astype(jnp.bfloat16)
    partial_value = lax.dot_general(
        hidden,
        lax.all_gather(down_weight, "dp", axis=0, tiled=True),
        (((1,), (1,)), ((), ())),
        preferred_element_type=jnp.float32,
    )
    feature_offset = lax.axis_index("mp") * local_width
    summed = lax.psum(partial_value.astype(jnp.bfloat16), "mp").astype(jnp.float32)
    resid = frame_rows + summed + down_bias
    resid_mean = jnp.mean(resid, axis=-1, keepdims=True)
    resid_square = jnp.mean(resid * resid, axis=-1, keepdims=True)
    whole_scaled = (resid - resid_mean) * lax.rsqrt(
        resid_square - resid_mean * resid_mean + epsilon
    )
    scaled = lax.dynamic_slice_in_dim(whole_scaled, feature_offset, local_width, 1)
    final_rows = (scaled * final_gain + final_bias).reshape(clip_count, slot_count, local_width)
    frame_mask = (jnp.arange(slot_count, dtype=jnp.int32)[None, :] < frame_counts[:, None]).astype(
        jnp.float32
    )
    pooled = jnp.sum(final_rows * frame_mask[:, :, None], axis=1) / frame_counts[:, None].astype(
        jnp.float32
    )
    pooled = pooled.astype(jnp.bfloat16)
    raw = lax.psum(
        jnp.dot(pooled, projection, preferred_element_type=jnp.float32).astype(jnp.bfloat16), "mp"
    ).astype(jnp.float32)
    return loss_part(raw, captions, positives, logit_scale, logit_bias)


def solution(mesh):
    return jax.shard_map(
        on_device,
        mesh=mesh,
        in_specs=(
            P("dp", None, "mp"),
            P("dp"),
            P(),
            P(),
            P("dp", "mp"),
            P("mp"),
            P("dp", "mp"),
            P(),
            P("mp"),
            P("mp"),
            P("mp", None),
            P(("dp", "mp"), None),
            P("dp"),
            P(),
            P(),
        ),
        out_specs=(P("dp", None), P("dp", None), P(("dp", "mp"), None)),
        check_vma=False,
    )
```

```python
import jax
import jax.numpy as jnp
import numpy as np
from jax import lax
from jax.experimental import pallas as pl
from jax.experimental.pallas import tpu as pltpu
from jax.sharding import PartitionSpec as P

D = 1408
E = 1024
NY, NZ, NX, NM = 8, 4, 4, 4
MESH = pl.DeviceIdType.MESH
epsilon = 1e-06
F32 = jnp.float32
BF16 = jnp.bfloat16


def position():
    dp = lax.axis_index("dp")
    mp = lax.axis_index("mp")
    return dp // (NZ * NX), (dp // NX) % NZ, dp % NX, mp


def device(y, z, x, m):
    return ((y * NZ + z) * NX + x, m)


def peer_at(axis, step):
    y, z, x, m = position()
    if axis == "y":
        place = (y + step) % NY
        return device(place, z, x, m), place
    if axis == "z":
        place = (z + step) % NZ
        return device(y, place, x, m), place
    if axis == "x":
        place = (x + step) % NX
        return device(y, z, place, m), place
    place = (m + step) % NM
    return device(y, z, x, place), place


SIZES = {"y": NY, "z": NZ, "x": NX, "m": NM}


def greet():
    barrier = pltpu.get_barrier_semaphore()
    total = 0
    for axis, size in SIZES.items():
        for step in range(1, size):
            target, _ = peer_at(axis, step)
            pl.semaphore_signal(barrier, inc=1, device_id=target, device_id_type=MESH)
            total += 1
    pl.semaphore_wait(barrier, total)


class Links:
    def __init__(self, send_sems, recv_sems):
        self.send_sems, self.recv_sems = send_sems, recv_sems
        self.rows = 0
        self.sent = []

    def row(self):
        self.rows += 1
        return self.rows - 1

    def make(self, source, slot, row, send_index, recv_index, target):
        return pltpu.make_async_remote_copy(
            src_ref=source,
            dst_ref=slot,
            send_sem=self.send_sems.at[row, send_index],
            recv_sem=self.recv_sems.at[row, recv_index],
            device_id=target,
            device_id_type=MESH,
        )

    def send(self, source, slot, row, send_index, recv_index, target):
        copy = self.make(source, slot, row, send_index, recv_index, target)
        copy.start()
        self.sent.append(copy)

    def arrive(self, slot, row, recv_index, target):
        self.make(slot, slot, row, 0, recv_index, target).wait_recv()

    def finish(self):
        for copy in self.sent:
            copy.wait_send()


class Exchange:
    def __init__(self, links, axis, source, slots):
        self.links, self.axis, self.slots = links, axis, slots
        self.row = links.row()
        y, z, x, m = position()
        own = {"y": y, "z": z, "x": x, "m": m}[axis]
        for step in range(1, SIZES[axis]):
            target, place = peer_at(axis, step)
            links.send(source(place), slots.at[own], self.row, step, own, target)

    def wait(self):
        for step in range(1, SIZES[self.axis]):
            target, place = peer_at(self.axis, step)
            self.links.arrive(self.slots.at[place], self.row, place, target)


def one_hot(hit):
    return jnp.where(hit, F32(1.0), F32(0.0)).astype(BF16)


def dot(a, b):
    return jnp.dot(a, b, preferred_element_type=F32)


def dot_t(a, b):
    return lax.dot_general(a, b, (((1,), (1,)), ((), ())), preferred_element_type=F32)


def iota(shape, dim):
    return lax.broadcasted_iota(jnp.int32, shape, dim)


def gelu(v):
    return 0.5 * v * (1.0 + lax.erf(v * F32(0.7071067811865476)))


def step_kernel(
    frames_ref,
    weight_ref,
    up_shard_ref,
    down_shard_ref,
    feature_ref,
    norm_ref,
    up_bias_ref,
    final_ref,
    projection_ref,
    captions_ref,
    positives_ref,
    scalars_ref,
    embed_ref,
    video_ref,
    text_ref,
    shard_z,
    up_x,
    up_y,
    down_x,
    frames_all,
    normed,
    order,
    bias_rows,
    resid,
    chip_out,
    chip_in,
    pair_out,
    pair_in,
    pool_rows,
    pool_out,
    pool_in,
    pool_all,
    raw_in,
    text_z,
    text_rows,
    text_y,
    video_x,
    where_x,
    text_out,
    text_in,
    video_out,
    video_in,
    text_sum,
    text_part,
    text_last,
    mp_in,
    send_sems,
    recv_sems,
):
    y, z, x, m = position()
    half, core = m // 2, m % 2
    chip_mate = half * 2 + (1 - core)
    pair_mate = (1 - half) * 2 + core
    far_mate = (1 - half) * 2 + (1 - core)
    chip_id = device(y, z, x, chip_mate)
    pair_id = device(y, z, x, pair_mate)
    up_id, up_from = peer_at("y", 1)
    down_id, down_from = peer_at("y", NY - 1)
    right_id, right = peer_at("x", 1)
    left_id, left = peer_at("x", NX - 1)
    across = (x + 2) % NX
    scale = scalars_ref[0]
    bias = scalars_ref[1]
    links = Links(send_sems, recv_sems)
    greet()

    shard_z[z] = jnp.zeros((2, 16, 768), BF16)
    shard_z[z, 0, 0:11, :] = up_shard_ref[...]
    shard_z[z, 1, 0:11, :] = down_shard_ref[...]
    gather_shards = Exchange(links, "z", lambda place: shard_z.at[z], shard_z)
    frames_row = links.row()
    links.send(frames_ref, frames_all.at[m], frames_row, 0, 0, chip_id)
    caption_values = captions_ref[...].astype(F32)
    text_z[z] = caption_values * lax.rsqrt(
        jnp.sum(caption_values * caption_values, axis=-1, keepdims=True) + epsilon
    )
    gather_text_z = Exchange(links, "z", lambda place: text_z.at[z], text_z)
    where_x[x] = positives_ref[...]
    gather_where = Exchange(links, "x", lambda place: where_x.at[x], where_x)
    frames_all[m] = frames_ref[...]

    slot_of = iota((48, 64), 1)
    target_row = lax.shift_right_logical(slot_of, 4) * 11 + lax.bitwise_and(slot_of, 15)
    pack_z = one_hot((iota((48, 64), 0) == target_row) & (lax.bitwise_and(slot_of, 15) < 11))
    gather_shards.wait()
    up_x[x] = dot(pack_z, shard_z[:, 0].reshape(64, 768)).astype(BF16)
    gather_up_x = Exchange(links, "x", lambda place: up_x.at[x], up_x)
    down_x[x, y] = dot(pack_z, shard_z[:, 1].reshape(64, 768)).astype(BF16)

    offsets = [0, -1, 1, -2, 2, -3, 3, -4]
    ring_row, from_left, from_right, from_across = links.row(), links.row(), links.row(), links.row()
    send_right, send_left = from_left, from_right

    def block_y(k):
        return (y + offsets[k] + NY) % NY

    def pass_down(k):
        block = down_x.at[x, block_y(k)]
        if k == 0 or (k % 2 == 1 and k < 7):
            following = 1 if k == 0 else k + 2
            links.send(block, block, ring_row, following, following, up_id)
        if k == 0 or (k % 2 == 0 and k < 6):
            links.send(block, block, ring_row, k + 2, k + 2, down_id)
        links.send(block, block, send_right, k, k, right_id)
        links.send(block, block, send_left, k, k, left_id)

    def take_down(k):
        links.arrive(down_x.at[x, block_y(k)], ring_row, k, up_id)
        pass_down(k)

    def take_side(k):
        left_block = down_x.at[left, block_y(k)]
        right_block = down_x.at[right, block_y(k)]
        links.arrive(left_block, from_left, k, left_id)
        if k % 2 == 0:
            links.send(left_block, left_block, from_across, k, k, right_id)
        links.arrive(right_block, from_right, k, right_id)
        if k % 2 == 1:
            links.send(right_block, right_block, from_across, k, k, left_id)

    pass_down(0)
    links.send(frames_ref, frames_all.at[m], frames_row, 1, 1, pair_id)

    slot_of = iota((176, 192), 1)
    from_x = (slot_of >= 48).astype(jnp.int32) + (slot_of >= 96).astype(jnp.int32) + (
        slot_of >= 144
    ).astype(jnp.int32)
    inside = slot_of - 48 * from_x
    from_z = (inside >= 11).astype(jnp.int32) + (inside >= 22).astype(jnp.int32) + (
        inside >= 33
    ).astype(jnp.int32)
    target_row = (from_z * 4 + from_x) * 11 + inside - 11 * from_z
    pack_x = one_hot((iota((176, 192), 0) == target_row) & (inside < 44))
    gather_up_x.wait()
    up_y[y] = dot(pack_x, up_x[...].reshape(192, 768)).astype(BF16)
    up_right, up_left = links.row(), links.row()

    def ring_part(ref, block, step, rightwards):
        if step < 4:
            return ref.at[block]
        return ref.at[block, 0:96, :] if rightwards else ref.at[block, 96:176, :]

    def pass_up(step):
        ahead = ring_part(up_y, (y - (step - 1) + NY) % NY, step, True)
        links.send(ahead, ahead, up_right, step, step, up_id)
        behind = ring_part(up_y, (y + (step - 1)) % NY, step, False)
        links.send(behind, behind, up_left, step, step, down_id)

    def take_up(step):
        links.arrive(ring_part(up_y, (y - step + NY) % NY, step, True), up_right, step, up_id)
        links.arrive(ring_part(up_y, (y + step) % NY, step, False), up_left, step, down_id)
        if step < 4:
            pass_up(step + 1)

    pass_up(1)
    take_down(1)
    take_down(2)
    take_side(0)
    gather_text_z.wait()
    for slot in range(NZ):
        text_rows[4 * slot : 4 * slot + 4, :] = text_z[slot]
    text_y[y] = text_rows[...].astype(BF16)
    take_down(3)
    take_down(4)
    take_side(1)
    take_side(2)
    take_up(1)
    take_down(5)
    take_down(6)
    take_side(3)
    links.arrive(frames_all.at[pair_mate], frames_row, 1, pair_id)
    links.send(frames_all.at[pair_mate], frames_all.at[pair_mate], frames_row, 2, 2, chip_id)
    links.arrive(frames_all.at[chip_mate], frames_row, 0, chip_id)
    take_down(7)
    take_side(4)
    for quarter in range(NM):
        hit = iota((352, 1536), 0) + 352 * quarter == feature_ref[...]
        order[quarter] = one_hot(hit)
    take_side(5)
    take_up(2)
    links.arrive(frames_all.at[far_mate], frames_row, 2, chip_id)

    def normalise(step, carry):
        rows = pl.ds(pl.multiple_of(step * 32, 32), 32)
        values = [frames_all[quarter, rows, :].astype(F32) for quarter in range(NM)]
        total = sum(jnp.sum(v, axis=-1, keepdims=True) for v in values)
        squares = sum(jnp.sum(v * v, axis=-1, keepdims=True) for v in values)
        mean = total * F32(1.0 / D)
        factor = lax.rsqrt(squares * F32(1.0 / D) - mean * mean + epsilon)
        for quarter in range(NM):
            normed[quarter, rows, :] = (
                (values[quarter] - mean) * factor * norm_ref[quarter, 0:1, :]
                + norm_ref[quarter, 1:2, :]
            ).astype(BF16)
        return carry

    lax.fori_loop(0, 8, normalise, 0)
    take_side(6)
    take_side(7)
    lax.fori_loop(8, 16, normalise, 0)
    take_up(3)
    gather_text_y = Exchange(links, "y", lambda place: text_y.at[y], text_y)

    def rows_of(place):
        return pl.ds(pl.multiple_of(place * 128, 128), 128)

    own = jnp.zeros((128, 1536), F32)
    own_bias = jnp.zeros((16, 1536), F32)
    for quarter in range(NM):
        own += dot(frames_all[quarter, rows_of(m), :], order[quarter])
        bias_part = norm_ref[quarter, 2:3, :]
        bias_rows[...] = jnp.zeros((16, 352), F32)
        for piece in range(3):
            rounded = bias_part.astype(BF16).astype(F32)
            bias_rows[piece : piece + 1, :] = rounded
            bias_part = bias_part - rounded
        own_bias += dot(bias_rows[...].astype(BF16), order[quarter])
    resid[...] = own + jnp.sum(own_bias, axis=0, keepdims=True)
    take_up(4)
    for k in range(NY):
        links.arrive(down_x.at[across, block_y(k)], from_across, k, right_id)

    def hidden_of(place):
        total = jnp.broadcast_to(up_bias_ref[...], (128, 768))
        for quarter in range(NM):
            total += dot(
                normed[quarter, rows_of(place), :],
                up_y[2 * quarter : 2 * quarter + 2].reshape(352, 768),
            )
        return gelu(total).astype(BF16)

    def partial_sums(hidden, block):
        return dot_t(hidden, down_x[block].reshape(384, 768))

    chip_row, pair_row = links.row(), links.row()
    hidden = hidden_of(far_mate)
    for block in range(NX):
        chip_out[0, :, 384 * block : 384 * block + 384] = partial_sums(hidden, block).astype(BF16)
    links.send(chip_out.at[0], chip_in.at[0], chip_row, 0, 0, chip_id)
    hidden = hidden_of(pair_mate)
    links.arrive(chip_in.at[0], chip_row, 0, chip_id)
    for block in range(NX):
        lanes = slice(384 * block, 384 * block + 384)
        pair_out[:, lanes] = (
            partial_sums(hidden, block) + chip_in[0, :, lanes].astype(F32)
        ).astype(BF16)
    links.send(pair_out, pair_in, pair_row, 0, 0, pair_id)
    hidden = hidden_of(chip_mate)
    for block in range(NX):
        chip_out[1, :, 384 * block : 384 * block + 384] = partial_sums(hidden, block).astype(BF16)
    links.send(chip_out.at[1], chip_in.at[1], chip_row, 1, 1, chip_id)
    hidden = hidden_of(m)
    links.arrive(chip_in.at[1], chip_row, 1, chip_id)
    for block in range(NX):
        lanes = slice(384 * block, 384 * block + 384)
        resid[:, lanes] += partial_sums(hidden, block) + chip_in[1, :, lanes].astype(F32)
    gather_text_y.wait()
    gather_where.wait()
    links.arrive(pair_in, pair_row, 0, pair_id)

    pool_rows[...] = jnp.zeros((16, 1536), F32)
    for clip in range(4):
        rows = slice(32 * clip, 32 * clip + 32)
        values = resid[rows, :] + pair_in[rows, :].astype(F32)
        mean = jnp.sum(values, axis=-1, keepdims=True) * F32(1.0 / D)
        square = jnp.sum(values * values, axis=-1, keepdims=True) * F32(1.0 / D)
        factor = lax.rsqrt(square - mean * mean + epsilon)
        weight = weight_ref[pl.ds(pl.multiple_of(m * 128 + 32 * clip, 32), 32), 0:1]
        mixed = jnp.sum((values - mean) * (factor * weight), axis=0, keepdims=True)
        rounded = mixed.astype(BF16).astype(F32)
        pool_rows[clip : clip + 1, :] = rounded
        pool_rows[clip + 4 : clip + 5, :] = mixed - rounded
    packed = pool_rows[...].astype(BF16)
    for quarter in range(NM):
        natural = dot_t(packed, order[quarter])
        pool_out[quarter] = natural[0:4, :] + natural[4:8, :]
    pool_in[m] = pool_out[m]
    share_pool = Exchange(links, "m", lambda place: pool_out.at[place], pool_in)
    share_pool.wait()
    for slot in range(NM):
        pool_all[4 * slot : 4 * slot + 4, :] = pool_in[slot]
    pooled = (pool_all[...] * final_ref[0:1, :] + final_ref[1:2, :]).astype(BF16)
    raw_in[m] = dot(pooled, projection_ref[...]).astype(BF16)
    share_raw = Exchange(links, "m", lambda place: raw_in.at[m], raw_in)
    share_raw.wait()
    raw = raw_in[0].astype(F32)
    for slot in range(1, NM):
        raw += raw_in[slot].astype(F32)

    embed = raw * lax.rsqrt(jnp.sum(raw * raw, axis=-1, keepdims=True) + epsilon)
    embed_ref[...] = embed
    video_x[x] = embed.astype(BF16)
    gather_video = Exchange(links, "x", lambda place: video_x.at[x], video_x)
    column = iota((NX * 16, NY * 16), 1)
    owner = lax.shift_right_logical(column, 2)
    ids = (((owner * 4) + x) * 4 + m) * 4 + lax.bitwise_and(column, 3)
    labels = jnp.where(ids == where_x[...].reshape(NX * 16, 128), F32(1.0), F32(-1.0))
    text = text_y[...].reshape(NY * 16, E)
    gather_video.wait()
    video = video_x[...].reshape(NX * 16, E)
    logits = scale * dot_t(video, text) + bias
    pair_weights = -labels * lax.logistic(-labels * logits)
    turned = jnp.transpose(pair_weights).astype(BF16)
    text_out[...] = (scale * dot(turned, video)).astype(BF16).reshape(NY, 16, E)
    text_in[y] = text_out[y]
    reduce_text_y = Exchange(links, "y", lambda place: text_out.at[place], text_in)
    video_out[...] = (scale * dot(pair_weights.astype(BF16), text)).astype(BF16).reshape(NX, 16, E)
    video_in[x] = video_out[x]
    reduce_video_x = Exchange(links, "x", lambda place: video_out.at[place], video_in)

    reduce_video_x.wait()
    video_total = video_in[0].astype(F32)
    for slot in range(1, NX):
        video_total += video_in[slot].astype(F32)
    mp_in[m] = video_total.astype(BF16)
    share_video = Exchange(links, "m", lambda place: mp_in.at[m], mp_in)
    reduce_text_y.wait()
    text_total = text_in[0].astype(F32)
    for slot in range(1, NY):
        text_total += text_in[slot].astype(F32)
    text_sum[...] = text_total
    for slot in range(NZ):
        text_part[slot] = text_sum[4 * slot : 4 * slot + 4, :]
    text_last[z] = text_part[z]
    reduce_text_z = Exchange(links, "z", lambda place: text_part.at[place], text_last)
    share_video.wait()
    video_grad = mp_in[0].astype(F32)
    for slot in range(1, NM):
        video_grad += mp_in[slot].astype(F32)
    video_ref[...] = video_grad
    reduce_text_z.wait()
    text_grad = text_last[0]
    for slot in range(1, NZ):
        text_grad += text_last[slot]
    text_ref[...] = text_grad
    links.finish()


def arrival_order():
    feature = np.full((NX, NY, 48), -1, np.int32)
    for x in range(NX):
        for y in range(NY):
            for z in range(NZ):
                first = ((y * NZ + z) * NX + x) * 11
                feature[x, y, 11 * z : 11 * z + 11] = np.arange(first, first + 11)
    return feature.reshape(1, 1536)


def on_device(
    frames,
    frame_counts,
    norm_gain,
    norm_bias,
    up_weight,
    up_bias,
    down_weight,
    down_bias,
    final_gain,
    final_bias,
    projection,
    captions,
    positives,
    logit_scale,
    logit_bias,
):
    slots = jnp.arange(32, dtype=jnp.int32)[None, :]
    counts = frame_counts[:, None]
    weights = jnp.where(slots < counts, 1.0 / counts.astype(F32), 0.0)
    weights = jnp.broadcast_to(weights.reshape(512, 1), (512, 128))
    norm = jnp.stack([part.reshape(4, 352) for part in (norm_gain, norm_bias, down_bias)], axis=1)
    vmem = pl.BlockSpec(memory_space=pltpu.VMEM)
    smem = pl.BlockSpec(memory_space=pltpu.SMEM)
    return pl.pallas_call(
        step_kernel,
        out_shape=(
            jax.ShapeDtypeStruct((16, E), F32),
            jax.ShapeDtypeStruct((16, E), F32),
            jax.ShapeDtypeStruct((4, E), F32),
        ),
        in_specs=[vmem] * 11 + [smem],
        out_specs=(vmem, vmem, vmem),
        scratch_shapes=[
            pltpu.VMEM((NZ, 2, 16, 768), BF16),
            pltpu.VMEM((NX, 48, 768), BF16),
            pltpu.VMEM((NY, 176, 768), BF16),
            pltpu.VMEM((NX, NY, 48, 768), BF16),
            pltpu.VMEM((NM, 512, 352), BF16),
            pltpu.VMEM((NM, 512, 352), BF16),
            pltpu.VMEM((NM, 352, 1536), BF16),
            pltpu.VMEM((16, 352), F32),
            pltpu.VMEM((128, 1536), F32),
            pltpu.VMEM((2, 128, 1536), BF16),
            pltpu.VMEM((2, 128, 1536), BF16),
            pltpu.VMEM((128, 1536), BF16),
            pltpu.VMEM((128, 1536), BF16),
            pltpu.VMEM((16, 1536), F32),
            pltpu.VMEM((NM, 4, 352), F32),
            pltpu.VMEM((NM, 4, 352), F32),
            pltpu.VMEM((16, 352), F32),
            pltpu.VMEM((NM, 16, E), BF16),
            pltpu.VMEM((NZ, 4, E), F32),
            pltpu.VMEM((16, E), F32),
            pltpu.VMEM((NY, 16, E), BF16),
            pltpu.VMEM((NX, 16, E), BF16),
            pltpu.VMEM((NX, 16, 128), jnp.int32),
            pltpu.VMEM((NY, 16, E), BF16),
            pltpu.VMEM((NY, 16, E), BF16),
            pltpu.VMEM((NX, 16, E), BF16),
            pltpu.VMEM((NX, 16, E), BF16),
            pltpu.VMEM((16, E), F32),
            pltpu.VMEM((NZ, 4, E), F32),
            pltpu.VMEM((NZ, 4, E), F32),
            pltpu.VMEM((NM, 16, E), BF16),
            pltpu.SemaphoreType.DMA((24, 8)),
            pltpu.SemaphoreType.DMA((24, 8)),
        ],
        compiler_params=pltpu.CompilerParams(
            collective_id=0, has_side_effects=True, vmem_limit_bytes=56 * 1024 * 1024
        ),
    )(
        frames.reshape(512, 352),
        weights,
        up_weight,
        down_weight,
        jnp.asarray(arrival_order()),
        norm,
        up_bias.reshape(1, 768),
        jnp.stack([final_gain, final_bias]),
        projection,
        captions,
        jnp.broadcast_to(positives[:, None], (16, 128)),
        jnp.stack([logit_scale, logit_bias]),
    )


def solution(mesh):
    return jax.shard_map(
        on_device,
        mesh=mesh,
        in_specs=(
            P("dp", None, "mp"),
            P("dp"),
            P(),
            P(),
            P("dp", "mp"),
            P("mp"),
            P("dp", "mp"),
            P(),
            P("mp"),
            P("mp"),
            P("mp", None),
            P(("dp", "mp"), None),
            P("dp"),
            P(),
            P(),
        ),
        out_specs=(P("dp", None), P("dp", None), P(("dp", "mp"), None)),
        check_vma=False,
    )
```

```python
import jax
import jax.numpy as jnp
from jax import lax
from jax.experimental import pallas as pl
from jax.experimental.pallas import tpu as pltpu
from jax.sharding import PartitionSpec as P

D = 1408
E = 1024
NY, NZ, NX, NM = 8, 4, 4, 4
MESH = pl.DeviceIdType.MESH
epsilon = 1e-06
F32 = jnp.float32
BF16 = jnp.bfloat16


def position():
    dp = lax.axis_index("dp")
    mp = lax.axis_index("mp")
    return dp // (NZ * NX), (dp // NX) % NZ, dp % NX, mp


def device(y, z, x, m):
    return ((y * NZ + z) * NX + x, m)


def peer_at(axis, step):
    y, z, x, m = position()
    if axis == "y":
        place = (y + step) % NY
        return device(place, z, x, m), place
    if axis == "z":
        place = (z + step) % NZ
        return device(y, place, x, m), place
    if axis == "x":
        place = (x + step) % NX
        return device(y, z, place, m), place
    place = (m + step) % NM
    return device(y, z, x, place), place


SIZES = {"y": NY, "z": NZ, "x": NX, "m": NM}


def greet():
    barrier = pltpu.get_barrier_semaphore()
    total = 0
    for axis, size in SIZES.items():
        for step in range(1, size):
            target, _ = peer_at(axis, step)
            pl.semaphore_signal(barrier, inc=1, device_id=target, device_id_type=MESH)
            total += 1
    return total


class Links:
    def __init__(self, send_sems, recv_sems):
        self.send_sems, self.recv_sems = send_sems, recv_sems
        self.rows = 0
        self.sent = []

    def row(self):
        self.rows += 1
        return self.rows - 1

    def make(self, source, slot, row, send_index, recv_index, target):
        return pltpu.make_async_remote_copy(
            src_ref=source,
            dst_ref=slot,
            send_sem=self.send_sems.at[row, send_index],
            recv_sem=self.recv_sems.at[row, recv_index],
            device_id=target,
            device_id_type=MESH,
        )

    def send(self, source, slot, row, send_index, recv_index, target):
        copy = self.make(source, slot, row, send_index, recv_index, target)
        copy.start()
        self.sent.append(copy)

    def arrive(self, slot, row, recv_index, target):
        self.make(slot, slot, row, 0, recv_index, target).wait_recv()

    def finish(self):
        for copy in self.sent:
            copy.wait_send()


class Exchange:
    def __init__(self, links, axis, source, slots):
        self.links, self.axis, self.slots = links, axis, slots
        self.row = links.row()
        y, z, x, m = position()
        own = {"y": y, "z": z, "x": x, "m": m}[axis]
        for step in range(1, SIZES[axis]):
            target, place = peer_at(axis, step)
            links.send(source(place), slots.at[own], self.row, step, own, target)

    def wait(self):
        for step in range(1, SIZES[self.axis]):
            target, place = peer_at(self.axis, step)
            self.links.arrive(self.slots.at[place], self.row, place, target)


def one_hot(hit):
    return jnp.where(hit, F32(1.0), F32(0.0)).astype(BF16)


def dot(a, b):
    return jnp.dot(a, b, preferred_element_type=F32)


def dot_t(a, b):
    return lax.dot_general(a, b, (((1,), (1,)), ((), ())), preferred_element_type=F32)


def iota(shape, dim):
    return lax.broadcasted_iota(jnp.int32, shape, dim)


def gelu(v):
    return 0.5 * v * (1.0 + lax.erf(v * F32(0.7071067811865476)))


def step_kernel(
    frames_hbm,
    counts_hbm,
    norm_gain_hbm,
    norm_bias_hbm,
    up_shard_hbm,
    up_bias_hbm,
    down_shard_hbm,
    down_bias_hbm,
    final_gain_hbm,
    final_bias_hbm,
    projection_hbm,
    captions_hbm,
    positives_hbm,
    scale_hbm,
    bias_hbm,
    embed_ref,
    video_ref,
    text_ref,
    counts_ref,
    norm_gain_ref,
    norm_bias_ref,
    up_shard_ref,
    up_bias_ref,
    down_shard_ref,
    down_bias_ref,
    final_gain_ref,
    final_bias_ref,
    projection_ref,
    captions_ref,
    positives_ref,
    scale_ref,
    bias_ref,
    norm_rows,
    up_z,
    down_y,
    projection_rows,
    final_rows,
    hidden,
    partial,
    waiting,
    up_x,
    up_y,
    down_x,
    frames_all,
    normed,
    order,
    bias_rows,
    resid,
    chip_out,
    chip_in,
    pair_out,
    pair_in,
    pool_in,
    pool_all,
    raw_in,
    text_first,
    text_rows,
    text_z,
    video_x,
    where_x,
    text_out_y,
    text_in_y,
    text_out_z,
    text_in_z,
    video_out,
    video_in,
    text_sum_y,
    text_sum_z,
    text_part_y,
    text_part_z,
    text_last_y,
    text_last_z,
    mp_in,
    send_sems,
    recv_sems,
    load_sems,
):
    y, z, x, m = position()
    loads = [
        pltpu.make_async_copy(source, target, load_sems.at[index])
        for index, (source, target) in enumerate(
            (
                (up_shard_hbm, up_shard_ref),
                (down_shard_hbm, down_shard_ref),
                (frames_hbm, frames_all.at[m]),
                (captions_hbm, captions_ref),
                (positives_hbm, positives_ref),
                (counts_hbm, counts_ref),
                (norm_gain_hbm, norm_gain_ref),
                (norm_bias_hbm, norm_bias_ref),
                (up_bias_hbm, up_bias_ref),
                (down_bias_hbm, down_bias_ref),
                (final_gain_hbm, final_gain_ref),
                (final_bias_hbm, final_bias_ref),
                (scale_hbm, scale_ref),
                (bias_hbm, bias_ref),
                (projection_hbm, projection_ref),
            )
        )
    ]
    for load in loads:
        load.start()
    greeted = greet()
    half, core = m // 2, m % 2
    chip_mate = half * 2 + (1 - core)
    pair_mate = (1 - half) * 2 + core
    far_mate = (1 - half) * 2 + (1 - core)
    chip_id = device(y, z, x, chip_mate)
    pair_id = device(y, z, x, pair_mate)
    up_id, up_from = peer_at("y", 1)
    down_id, down_from = peer_at("y", NY - 1)
    right_id, right = peer_at("x", 1)
    left_id, left = peer_at("x", NX - 1)
    across = (x + 2) % NX
    links = Links(send_sems, recv_sems)
    loads[0].wait()
    loads[1].wait()
    up_z[z] = jnp.zeros((16, 768), BF16)
    up_z[z, 0:11, :] = up_shard_ref[...]
    down_y[y] = jnp.zeros((16, 768), BF16)
    down_y[y, 0:11, :] = down_shard_ref[...]
    for load in loads[2:]:
        load.wait()
    caption_values = captions_ref[...].astype(F32)
    text_first[y] = caption_values * lax.rsqrt(
        jnp.sum(caption_values * caption_values, axis=-1, keepdims=True) + epsilon
    )
    for row in range(16):
        where_x[x, row : row + 1, :] = jnp.full((1, 128), positives_ref[row], jnp.int32)
    scale = scale_ref[0]
    bias = bias_ref[0]
    for row, vector in enumerate((norm_gain_ref, norm_bias_ref, down_bias_ref)):
        norm_rows[row : row + 1, :] = vector[...].reshape(1, D)
    pl.semaphore_wait(pltpu.get_barrier_semaphore(), greeted)

    gather_up_z = Exchange(links, "z", lambda place: up_z.at[z], up_z)
    gather_down_y = Exchange(links, "y", lambda place: down_y.at[y], down_y)
    frames_row = links.row()
    links.send(frames_all.at[m], frames_all.at[m], frames_row, 0, 0, chip_id)
    gather_text_first = Exchange(links, "y", lambda place: text_first.at[y], text_first)

    def feature_at(position_of):
        from_x = sum((position_of >= 384 * k).astype(jnp.int32) for k in range(1, NX))
        inside = position_of - 384 * from_x
        from_z = sum((inside >= 96 * k).astype(jnp.int32) for k in range(1, NZ))
        inside = inside - 96 * from_z
        from_y = sum((inside >= 11 * k).astype(jnp.int32) for k in range(1, NY))
        feature = ((from_y * NZ + from_z) * NX + from_x) * 11 + inside - 11 * from_y
        return jnp.where(inside < 88, feature, -1)

    feature = feature_at(iota((1, 1536), 1))
    for quarter in range(NM):
        order[quarter] = one_hot(iota((352, 1536), 0) + 352 * quarter == feature)

    def pack(rows, slots):
        slot_of = iota((rows, slots), 1)
        target_row = lax.shift_right_logical(slot_of, 4) * 11 + lax.bitwise_and(slot_of, 15)
        return one_hot((iota((rows, slots), 0) == target_row) & (lax.bitwise_and(slot_of, 15) < 11))

    gather_up_z.wait()
    up_x[x] = dot(pack(48, 64), up_z[...].reshape(64, 768)).astype(BF16)
    gather_up_x = Exchange(links, "x", lambda place: up_x.at[x], up_x)
    pair_rows = (links.row(), links.row())

    def frame_chunk(place, chunk):
        return frames_all.at[place, 128 * chunk : 128 * chunk + 128, :]

    def send_frames(chunk):
        links.send(frame_chunk(m, chunk), frame_chunk(m, chunk), pair_rows[0], chunk, chunk, pair_id)

    def take_frames(chunk):
        block = frame_chunk(pair_mate, chunk)
        links.arrive(block, pair_rows[0], chunk, pair_id)
        links.send(block, block, pair_rows[1], chunk, chunk, chip_id)

    send_frames(0)

    gather_down_y.wait()
    down_x[x, z] = dot(pack(96, 128), down_y[...].reshape(128, 768)).astype(BF16)
    above_id, above = peer_at("z", 1)
    below_id, below = peer_at("z", NZ - 1)
    from_below, from_above, from_far = links.row(), links.row(), links.row()
    from_left, from_right, from_across = links.row(), links.row(), links.row()

    def piece(column, k):
        place = (z + (0, 1, 3, 2)[k // 2]) % NZ
        return down_x.at[column, place, 48 * (k % 2) : 48 * (k % 2) + 48, :]

    def pass_down(k):
        for part in (2 * k, 2 * k + 1):
            links.send(piece(x, part), piece(x, part), from_left, part, part, right_id)
            links.send(piece(x, part), piece(x, part), from_right, part, part, left_id)

    def take_down(k):
        first, second = piece(x, 2 * k), piece(x, 2 * k + 1)
        row = (None, from_above, from_below, from_far)[k]
        links.arrive(first, row, 0, above_id)
        links.arrive(second, row, 1, above_id)
        if k == 1:
            links.send(second, second, from_far, 1, 1, below_id)
        if k == 2:
            links.send(first, first, from_far, 0, 0, above_id)
        pass_down(k)

    def take_side(k):
        links.arrive(piece(left, k), from_left, k, left_id)
        if k % 2 == 0:
            links.send(piece(left, k), piece(left, k), from_across, k, k, right_id)
        links.arrive(piece(right, k), from_right, k, right_id)
        if k % 2 == 1:
            links.send(piece(right, k), piece(right, k), from_across, k, k, left_id)

    for part in range(2):
        links.send(piece(x, part), piece(x, part), from_below, part, part, above_id)
        links.send(piece(x, part), piece(x, part), from_above, part, part, below_id)
    pass_down(0)
    gather_where = Exchange(links, "x", lambda place: where_x.at[x], where_x)

    slot_of = iota((176, 192), 1)
    from_x = (slot_of >= 48).astype(jnp.int32) + (slot_of >= 96).astype(jnp.int32) + (
        slot_of >= 144
    ).astype(jnp.int32)
    inside = slot_of - 48 * from_x
    from_z = (inside >= 11).astype(jnp.int32) + (inside >= 22).astype(jnp.int32) + (
        inside >= 33
    ).astype(jnp.int32)
    target_row = (from_z * 4 + from_x) * 11 + inside - 11 * from_z
    pack_x = one_hot((iota((176, 192), 0) == target_row) & (inside < 44))
    gather_up_x.wait()
    up_y[y] = dot(pack_x, up_x[...].reshape(192, 768)).astype(BF16)
    up_right, up_left = (links.row(), links.row()), (links.row(), links.row())

    def pass_up(step, part):
        rows = slice(0, 96) if part == 0 else slice(96, 176)
        if step < 4 or part == 0:
            ahead = up_y.at[(y - (step - 1) + NY) % NY, rows, :]
            links.send(ahead, ahead, up_right[part], step, step, up_id)
        if step < 4 or part == 1:
            behind = up_y.at[(y + (step - 1)) % NY, rows, :]
            links.send(behind, behind, up_left[part], step, step, down_id)

    def take_up(step, part):
        rows = slice(0, 96) if part == 0 else slice(96, 176)
        if step < 4 or part == 0:
            links.arrive(up_y.at[(y - step + NY) % NY, rows, :], up_right[part], step, up_id)
        if step < 4 or part == 1:
            links.arrive(up_y.at[(y + step) % NY, rows, :], up_left[part], step, down_id)
        if step < 4:
            pass_up(step + 1, part)

    pass_up(1, 0)
    pass_up(1, 1)
    gather_text_first.wait()
    for slot in range(NY):
        text_rows[4 * slot : 4 * slot + 4, :] = text_first[slot]
    text_z[z] = text_rows[...].astype(BF16)
    take_side(0)
    take_side(1)
    take_down(1)
    take_down(2)
    send_frames(1)
    send_frames(2)
    send_frames(3)
    take_up(1, 0)
    take_side(2)
    take_down(3)
    take_up(1, 1)
    take_side(3)
    take_frames(0)
    take_up(2, 0)
    take_side(4)
    take_frames(1)
    links.arrive(frames_all.at[chip_mate], frames_row, 0, chip_id)

    def normalise(step, carry):
        rows = pl.ds(pl.multiple_of(step * 32, 32), 32)
        values = [frames_all[quarter, rows, :].astype(F32) for quarter in range(NM)]
        total = sum(jnp.sum(v, axis=-1, keepdims=True) for v in values)
        squares = sum(jnp.sum(v * v, axis=-1, keepdims=True) for v in values)
        mean = total * F32(1.0 / D)
        factor = lax.rsqrt(squares * F32(1.0 / D) - mean * mean + epsilon)
        for quarter in range(NM):
            normed[quarter, rows, :] = (
                (values[quarter] - mean) * factor * norm_rows[0:1, 352 * quarter : 352 * quarter + 352]
                + norm_rows[1:2, 352 * quarter : 352 * quarter + 352]
            ).astype(BF16)
        return carry

    def normalise_chunk(chunk):
        links.arrive(frame_chunk(far_mate, chunk), pair_rows[1], chunk, chip_id)
        lax.fori_loop(4 * chunk, 4 * chunk + 4, normalise, 0)

    normalise_chunk(0)
    take_side(5)
    take_up(2, 1)
    take_frames(2)
    normalise_chunk(1)
    take_side(6)
    take_up(3, 0)
    take_frames(3)
    gather_text_z = Exchange(links, "z", lambda place: text_z.at[z], text_z)
    normalise_chunk(2)
    take_side(7)
    take_up(3, 1)
    normalise_chunk(3)

    def rows_of(place):
        return pl.ds(pl.multiple_of(place * 128, 128), 128)

    own = jnp.zeros((128, 1536), F32)
    own_bias = jnp.zeros((16, 1536), F32)
    for quarter in range(NM):
        own += dot(frames_all[quarter, rows_of(m), :], order[quarter])
        bias_part = norm_rows[2:3, 352 * quarter : 352 * quarter + 352]
        bias_rows[...] = jnp.zeros((16, 352), F32)
        for digit in range(3):
            rounded = bias_part.astype(BF16).astype(F32)
            bias_rows[digit : digit + 1, :] = rounded
            bias_part = bias_part - rounded
        own_bias += dot(bias_rows[...].astype(BF16), order[quarter])
    own = own + jnp.sum(own_bias, axis=0, keepdims=True)
    for block in range(NX):
        resid[block] = own[:, 384 * block : 384 * block + 384]
    turn = one_hot(iota((1536, 352), 1) + 352 * m == feature_at(iota((1536, 1), 0)))
    projection_rows[...] = dot(turn, projection_ref[...]).astype(BF16)
    bias_rows[...] = jnp.zeros((16, 352), F32)
    for row, vector in enumerate((final_gain_ref, final_bias_ref)):
        rest = vector[...].reshape(1, 352)
        for part in range(3):
            rounded = rest.astype(BF16).astype(F32)
            bias_rows[3 * row + part : 3 * row + part + 1, :] = rounded
            rest = rest - rounded
    final_parts = dot(bias_rows[...].astype(BF16), order[m])
    final_rows[0:1, :] = jnp.sum(final_parts[0:3, :], axis=0, keepdims=True)
    final_rows[1:2, :] = jnp.sum(final_parts[3:6, :], axis=0, keepdims=True)
    take_up(4, 0)
    take_up(4, 1)
    arrival = [x, left, right, across]

    def hidden_of(side):
        rows = pl.ds(pl.multiple_of(side * 256, 256), 256)
        total = jnp.broadcast_to(up_bias_ref[...].reshape(1, 768), (256, 768))
        for quarter in range(NM):
            total += dot(
                normed[quarter, rows, :],
                up_y[2 * quarter : 2 * quarter + 2].reshape(352, 768),
            )
        hidden[...] = gelu(total).astype(BF16)

    def partial_sums(block):
        sums = dot_t(hidden[...], down_x[block].reshape(384, 768))
        partial[0] = sums[0:128]
        partial[1] = sums[128:256]

    chip_rows, pair_row = (links.row(), links.row()), links.row()

    def pass_pair(k):
        links.arrive(chip_in.at[0, k], chip_rows[0], k, chip_id)
        pair_out[k] = (waiting[k] + chip_in[0, k].astype(F32)).astype(BF16)
        links.send(pair_out.at[k], pair_in.at[k], pair_row, k, k, pair_id)

    hidden_of(1 - half)
    for k, block in enumerate(arrival):
        if k == 3:
            for part in range(2 * NZ):
                links.arrive(piece(across, part), from_across, part, right_id)
        partial_sums(block)
        chip_out[0, k] = partial[1 - core].astype(BF16)
        links.send(chip_out.at[0, k], chip_in.at[0, k], chip_rows[0], k, k, chip_id)
        waiting[k] = partial[core]
        if k > 0:
            pass_pair(k - 1)
    pass_pair(3)
    hidden_of(half)
    for k, block in enumerate(arrival):
        partial_sums(block)
        chip_out[1, k] = partial[1 - core].astype(BF16)
        links.send(chip_out.at[1, k], chip_in.at[1, k], chip_rows[1], k, k, chip_id)
        resid[block] += partial[core]
    for k, block in enumerate(arrival):
        links.arrive(chip_in.at[1, k], chip_rows[1], k, chip_id)
        resid[block] += chip_in[1, k].astype(F32)
    gather_text_z.wait()
    gather_where.wait()
    for k, block in enumerate(arrival):
        links.arrive(pair_in.at[k], pair_row, k, pair_id)
        resid[block] += pair_in[k].astype(F32)

    for clip in range(4):
        rows = slice(32 * clip, 32 * clip + 32)
        values = [resid[block, rows, :] for block in range(NX)]
        total = sum(jnp.sum(v, axis=-1, keepdims=True) for v in values)
        squares = sum(jnp.sum(v * v, axis=-1, keepdims=True) for v in values)
        mean = total * F32(1.0 / D)
        factor = lax.rsqrt(squares * F32(1.0 / D) - mean * mean + epsilon)
        count = jnp.full((32, 1), counts_ref[m * 4 + clip], jnp.int32)
        weight = jnp.where(iota((32, 1), 0) < count, factor / count.astype(F32), F32(0.0))
        for block in range(NX):
            lanes = slice(384 * block, 384 * block + 384)
            pool_in[m, clip : clip + 1, lanes] = jnp.sum(
                (values[block] - mean) * weight, axis=0, keepdims=True
            )
    share_pool = Exchange(links, "m", lambda place: pool_in.at[m], pool_in)
    share_pool.wait()
    for slot in range(NM):
        pool_all[4 * slot : 4 * slot + 4, :] = pool_in[slot]
    pooled = (pool_all[...] * final_rows[0:1, :] + final_rows[1:2, :]).astype(BF16)
    raw_in[m] = dot(pooled, projection_rows[...]).astype(BF16)
    share_raw = Exchange(links, "m", lambda place: raw_in.at[m], raw_in)
    share_raw.wait()
    raw = raw_in[0].astype(F32)
    for slot in range(1, NM):
        raw += raw_in[slot].astype(F32)

    embed = raw * lax.rsqrt(jnp.sum(raw * raw, axis=-1, keepdims=True) + epsilon)
    embed_ref[...] = embed
    video_x[x] = embed.astype(BF16)
    gather_video = Exchange(links, "x", lambda place: video_x.at[x], video_x)
    column = iota((NX * 16, NY * 16), 1)
    owner = lax.bitwise_and(lax.shift_right_logical(column, 2), 7) * NZ + lax.shift_right_logical(column, 5)
    ids = (((owner * 4) + x) * 4 + m) * 4 + lax.bitwise_and(column, 3)
    labels = jnp.where(ids == where_x[...].reshape(NX * 16, 128), F32(1.0), F32(-1.0))
    text = text_z[...].reshape(NY * 16, E)
    row_of = iota((128, 128), 0)
    moved = (
        lax.bitwise_and(lax.shift_right_logical(row_of, 2), 3) * 32
        + lax.shift_right_logical(row_of, 4) * 4
        + lax.bitwise_and(row_of, 3)
    )
    reorder = one_hot(iota((128, 128), 1) == moved)
    gather_video.wait()
    video = video_x[...].reshape(NX * 16, E)
    logits = scale * dot_t(video, text) + bias
    pair_weights = -labels * lax.logistic(-labels * logits)
    turned = jnp.transpose(pair_weights).astype(BF16)
    by_y = dot(reorder, turned).astype(BF16)
    text_out_y[...] = (scale * dot(by_y, video[:, 0:512])).astype(BF16).reshape(NY, 16, 512)
    text_in_y[y] = text_out_y[y]
    reduce_first_y = Exchange(links, "y", lambda place: text_out_y.at[place], text_in_y)
    text_out_z[...] = (scale * dot(turned, video[:, 512:1024])).astype(BF16).reshape(NZ, 32, 512)
    text_in_z[z] = text_out_z[z]
    reduce_first_z = Exchange(links, "z", lambda place: text_out_z.at[place], text_in_z)
    video_out[...] = (scale * dot(pair_weights.astype(BF16), text)).astype(BF16).reshape(NX, 16, E)
    video_in[x] = video_out[x]
    reduce_video_x = Exchange(links, "x", lambda place: video_out.at[place], video_in)

    reduce_video_x.wait()
    video_total = video_in[0].astype(F32)
    for slot in range(1, NX):
        video_total += video_in[slot].astype(F32)
    mp_in[m] = video_total.astype(BF16)
    share_video = Exchange(links, "m", lambda place: mp_in.at[m], mp_in)
    reduce_first_z.wait()
    text_total = text_in_z[0].astype(F32)
    for slot in range(1, NZ):
        text_total += text_in_z[slot].astype(F32)
    text_sum_z[...] = text_total
    for slot in range(NY):
        text_part_y[slot] = text_sum_z[4 * slot : 4 * slot + 4, :]
    text_last_y[y] = text_part_y[y]
    reduce_last_y = Exchange(links, "y", lambda place: text_part_y.at[place], text_last_y)
    reduce_first_y.wait()
    text_total = text_in_y[0].astype(F32)
    for slot in range(1, NY):
        text_total += text_in_y[slot].astype(F32)
    text_sum_y[...] = text_total
    for slot in range(NZ):
        text_part_z[slot] = text_sum_y[4 * slot : 4 * slot + 4, :]
    text_last_z[z] = text_part_z[z]
    reduce_last_z = Exchange(links, "z", lambda place: text_part_z.at[place], text_last_z)
    share_video.wait()
    video_grad = mp_in[0].astype(F32)
    for slot in range(1, NM):
        video_grad += mp_in[slot].astype(F32)
    video_ref[...] = video_grad
    reduce_last_y.wait()
    text_grad = text_last_y[0]
    for slot in range(1, NY):
        text_grad += text_last_y[slot]
    text_ref[:, 512:1024] = text_grad
    reduce_last_z.wait()
    text_grad = text_last_z[0]
    for slot in range(1, NZ):
        text_grad += text_last_z[slot]
    text_ref[:, 0:512] = text_grad
    links.finish()


def on_device(
    frames,
    frame_counts,
    norm_gain,
    norm_bias,
    up_weight,
    up_bias,
    down_weight,
    down_bias,
    final_gain,
    final_bias,
    projection,
    captions,
    positives,
    logit_scale,
    logit_bias,
):
    vmem = pl.BlockSpec(memory_space=pltpu.VMEM)
    hbm = pl.BlockSpec(memory_space=pltpu.HBM)
    return pl.pallas_call(
        step_kernel,
        out_shape=(
            jax.ShapeDtypeStruct((16, E), F32),
            jax.ShapeDtypeStruct((16, E), F32),
            jax.ShapeDtypeStruct((4, E), F32),
        ),
        in_specs=[hbm] * 15,
        out_specs=(vmem, vmem, vmem),
        scratch_shapes=[
            pltpu.SMEM((16,), jnp.int32),
            pltpu.VMEM((D,), F32),
            pltpu.VMEM((D,), F32),
            pltpu.VMEM((11, 768), BF16),
            pltpu.VMEM((768,), F32),
            pltpu.VMEM((11, 768), BF16),
            pltpu.VMEM((D,), F32),
            pltpu.VMEM((352,), F32),
            pltpu.VMEM((352,), F32),
            pltpu.VMEM((352, E), BF16),
            pltpu.VMEM((4, E), BF16),
            pltpu.SMEM((16,), jnp.int32),
            pltpu.SMEM((1,), F32),
            pltpu.SMEM((1,), F32),
            pltpu.VMEM((8, D), F32),
            pltpu.VMEM((NZ, 16, 768), BF16),
            pltpu.VMEM((NY, 16, 768), BF16),
            pltpu.VMEM((1536, E), BF16),
            pltpu.VMEM((8, 1536), F32),
            pltpu.VMEM((256, 768), BF16),
            pltpu.VMEM((2, 128, 384), F32),
            pltpu.VMEM((NX, 128, 384), F32),
            pltpu.VMEM((NX, 48, 768), BF16),
            pltpu.VMEM((NY, 176, 768), BF16),
            pltpu.VMEM((NX, NZ, 96, 768), BF16),
            pltpu.VMEM((NM, 512, 352), BF16),
            pltpu.VMEM((NM, 512, 352), BF16),
            pltpu.VMEM((NM, 352, 1536), BF16),
            pltpu.VMEM((16, 352), F32),
            pltpu.VMEM((NX, 128, 384), F32),
            pltpu.VMEM((2, NX, 128, 384), BF16),
            pltpu.VMEM((2, NX, 128, 384), BF16),
            pltpu.VMEM((NX, 128, 384), BF16),
            pltpu.VMEM((NX, 128, 384), BF16),
            pltpu.VMEM((NM, 4, 1536), F32),
            pltpu.VMEM((16, 1536), F32),
            pltpu.VMEM((NM, 16, E), BF16),
            pltpu.VMEM((NY, 4, E), F32),
            pltpu.VMEM((32, E), F32),
            pltpu.VMEM((NZ, 32, E), BF16),
            pltpu.VMEM((NX, 16, E), BF16),
            pltpu.VMEM((NX, 16, 128), jnp.int32),
            pltpu.VMEM((NY, 16, 512), BF16),
            pltpu.VMEM((NY, 16, 512), BF16),
            pltpu.VMEM((NZ, 32, 512), BF16),
            pltpu.VMEM((NZ, 32, 512), BF16),
            pltpu.VMEM((NX, 16, E), BF16),
            pltpu.VMEM((NX, 16, E), BF16),
            pltpu.VMEM((16, 512), F32),
            pltpu.VMEM((32, 512), F32),
            pltpu.VMEM((NY, 4, 512), F32),
            pltpu.VMEM((NZ, 4, 512), F32),
            pltpu.VMEM((NY, 4, 512), F32),
            pltpu.VMEM((NZ, 4, 512), F32),
            pltpu.VMEM((NM, 16, E), BF16),
            pltpu.SemaphoreType.DMA((36, 8)),
            pltpu.SemaphoreType.DMA((36, 8)),
            pltpu.SemaphoreType.DMA((15,)),
        ],
        compiler_params=pltpu.CompilerParams(
            collective_id=0, has_side_effects=True, vmem_limit_bytes=56 * 1024 * 1024
        ),
    )(
        frames.reshape(512, 352),
        frame_counts,
        norm_gain,
        norm_bias,
        up_weight,
        up_bias,
        down_weight,
        down_bias,
        final_gain,
        final_bias,
        projection,
        captions,
        positives,
        logit_scale.reshape(1),
        logit_bias.reshape(1),
    )


def solution(mesh):
    return jax.shard_map(
        on_device,
        mesh=mesh,
        in_specs=(
            P("dp", None, "mp"),
            P("dp"),
            P(),
            P(),
            P("dp", "mp"),
            P("mp"),
            P("dp", "mp"),
            P(),
            P("mp"),
            P("mp"),
            P("mp", None),
            P(("dp", "mp"), None),
            P("dp"),
            P(),
            P(),
        ),
        out_specs=(P("dp", None), P("dp", None), P(("dp", "mp"), None)),
        check_vma=False,
    )
```

```python
import jax
import jax.numpy as jnp
from jax import lax
from jax.experimental import pallas as pl
from jax.experimental.pallas import tpu as pltpu
from jax.sharding import PartitionSpec as P

D = 1408
E = 1024
NY, NZ, NX, NM = 8, 4, 4, 4
MESH = pl.DeviceIdType.MESH
epsilon = 1e-06
F32 = jnp.float32
BF16 = jnp.bfloat16


def position():
    dp = lax.axis_index("dp")
    mp = lax.axis_index("mp")
    return dp // (NZ * NX), (dp // NX) % NZ, dp % NX, mp


def device(y, z, x, m):
    return ((y * NZ + z) * NX + x, m)


def peer_at(axis, step):
    y, z, x, m = position()
    if axis == "y":
        place = (y + step) % NY
        return device(place, z, x, m), place
    if axis == "z":
        place = (z + step) % NZ
        return device(y, place, x, m), place
    if axis == "x":
        place = (x + step) % NX
        return device(y, z, place, m), place
    place = (m + step) % NM
    return device(y, z, x, place), place


SIZES = {"y": NY, "z": NZ, "x": NX, "m": NM}


def greet():
    barrier = pltpu.get_barrier_semaphore()
    total = 0
    for axis, size in SIZES.items():
        for step in range(1, size):
            target, _ = peer_at(axis, step)
            pl.semaphore_signal(barrier, inc=1, device_id=target, device_id_type=MESH)
            total += 1
    return total


class Links:
    def __init__(self, send_sems, recv_sems):
        self.send_sems, self.recv_sems = send_sems, recv_sems
        self.rows = 0
        self.sent = []

    def row(self):
        self.rows += 1
        return self.rows - 1

    def make(self, source, slot, row, send_index, recv_index, target):
        return pltpu.make_async_remote_copy(
            src_ref=source,
            dst_ref=slot,
            send_sem=self.send_sems.at[row, send_index],
            recv_sem=self.recv_sems.at[row, recv_index],
            device_id=target,
            device_id_type=MESH,
        )

    def send(self, source, slot, row, send_index, recv_index, target):
        copy = self.make(source, slot, row, send_index, recv_index, target)
        copy.start()
        self.sent.append(copy)

    def arrive(self, slot, row, recv_index, target):
        self.make(slot, slot, row, 0, recv_index, target).wait_recv()

    def finish(self):
        for copy in self.sent:
            copy.wait_send()


class Exchange:
    def __init__(self, links, axis, source, slots):
        self.links, self.axis, self.slots = links, axis, slots
        self.row = links.row()
        y, z, x, m = position()
        own = {"y": y, "z": z, "x": x, "m": m}[axis]
        for step in range(1, SIZES[axis]):
            target, place = peer_at(axis, step)
            links.send(source(place), slots.at[own], self.row, step, own, target)

    def wait(self):
        for step in range(1, SIZES[self.axis]):
            target, place = peer_at(self.axis, step)
            self.links.arrive(self.slots.at[place], self.row, place, target)


def one_hot(hit):
    return jnp.where(hit, F32(1.0), F32(0.0)).astype(BF16)


def dot(a, b):
    return jnp.dot(a, b, preferred_element_type=F32)


def dot_t(a, b):
    return lax.dot_general(a, b, (((1,), (1,)), ((), ())), preferred_element_type=F32)


def iota(shape, dim):
    return lax.broadcasted_iota(jnp.int32, shape, dim)


def gelu(v):
    return 0.5 * v * (1.0 + lax.erf(v * F32(0.7071067811865476)))


def step_kernel(
    frames_hbm,
    counts_hbm,
    norm_gain_hbm,
    norm_bias_hbm,
    up_shard_hbm,
    up_bias_hbm,
    down_shard_hbm,
    down_bias_hbm,
    final_gain_hbm,
    final_bias_hbm,
    projection_hbm,
    captions_hbm,
    positives_hbm,
    scale_hbm,
    bias_hbm,
    embed_ref,
    video_ref,
    text_ref,
    counts_ref,
    norm_gain_ref,
    norm_bias_ref,
    up_shard_ref,
    up_bias_ref,
    down_shard_ref,
    down_bias_ref,
    final_gain_ref,
    final_bias_ref,
    projection_ref,
    captions_ref,
    positives_ref,
    scale_ref,
    bias_ref,
    norm_rows,
    up_z,
    down_y,
    projection_rows,
    final_rows,
    hidden,
    partial,
    waiting,
    up_x,
    up_y,
    down_x,
    frames_all,
    normed,
    order,
    bias_rows,
    resid,
    chip_out,
    chip_in,
    pair_out,
    pair_in,
    pool_in,
    pool_all,
    raw_in,
    text_first,
    text_rows,
    text_z,
    video_x,
    where_x,
    text_out_y,
    text_in_y,
    text_out_z,
    text_in_z,
    video_out,
    video_in,
    text_sum_y,
    text_sum_z,
    text_part_y,
    text_part_z,
    text_last_y,
    text_last_z,
    mp_in,
    send_sems,
    recv_sems,
    load_sems,
):
    y, z, x, m = position()
    loads = [
        pltpu.make_async_copy(source, target, load_sems.at[index])
        for index, (source, target) in enumerate(
            (
                (up_shard_hbm, up_shard_ref),
                (down_shard_hbm, down_shard_ref),
                (frames_hbm, frames_all.at[m]),
                (captions_hbm, captions_ref),
                (positives_hbm, positives_ref),
                (counts_hbm, counts_ref),
                (norm_gain_hbm, norm_gain_ref),
                (norm_bias_hbm, norm_bias_ref),
                (up_bias_hbm, up_bias_ref),
                (down_bias_hbm, down_bias_ref),
                (final_gain_hbm, final_gain_ref),
                (final_bias_hbm, final_bias_ref),
                (scale_hbm, scale_ref),
                (bias_hbm, bias_ref),
                (projection_hbm, projection_ref),
            )
        )
    ]
    loads[0].start()
    loads[1].start()
    greeted = greet()
    for load in loads[2:]:
        load.start()
    half, core = m // 2, m % 2
    chip_mate = half * 2 + (1 - core)
    pair_mate = (1 - half) * 2 + core
    far_mate = (1 - half) * 2 + (1 - core)
    chip_id = device(y, z, x, chip_mate)
    pair_id = device(y, z, x, pair_mate)
    up_id, up_from = peer_at("y", 1)
    down_id, down_from = peer_at("y", NY - 1)
    right_id, right = peer_at("x", 1)
    left_id, left = peer_at("x", NX - 1)
    across = (x + 2) % NX
    links = Links(send_sems, recv_sems)
    loads[0].wait()
    loads[1].wait()
    up_z[z] = jnp.zeros((16, 768), BF16)
    up_z[z, 0:11, :] = up_shard_ref[...]
    down_y[y] = jnp.zeros((16, 768), BF16)
    down_y[y, 0:11, :] = down_shard_ref[...]
    pl.semaphore_wait(pltpu.get_barrier_semaphore(), greeted)

    gather_up_z = Exchange(links, "z", lambda place: up_z.at[z], up_z)
    gather_down_y = Exchange(links, "y", lambda place: down_y.at[y], down_y)
    for load in loads[2:]:
        load.wait()
    caption_values = captions_ref[...].astype(F32)
    text_first[y] = caption_values * lax.rsqrt(
        jnp.sum(caption_values * caption_values, axis=-1, keepdims=True) + epsilon
    )
    for row in range(16):
        where_x[x, row : row + 1, :] = jnp.full((1, 128), positives_ref[row], jnp.int32)
    scale = scale_ref[0]
    bias = bias_ref[0]
    for row, vector in enumerate((norm_gain_ref, norm_bias_ref, down_bias_ref)):
        norm_rows[row : row + 1, :] = vector[...].reshape(1, D)
    frames_row = links.row()
    links.send(frames_all.at[m], frames_all.at[m], frames_row, 0, 0, chip_id)

    def feature_at(position_of):
        from_x = sum((position_of >= 384 * k).astype(jnp.int32) for k in range(1, NX))
        inside = position_of - 384 * from_x
        from_z = sum((inside >= 96 * k).astype(jnp.int32) for k in range(1, NZ))
        inside = inside - 96 * from_z
        from_y = sum((inside >= 11 * k).astype(jnp.int32) for k in range(1, NY))
        feature = ((from_y * NZ + from_z) * NX + from_x) * 11 + inside - 11 * from_y
        return jnp.where(inside < 88, feature, -1)

    def pack(rows, slots):
        slot_of = iota((rows, slots), 1)
        target_row = lax.shift_right_logical(slot_of, 4) * 11 + lax.bitwise_and(slot_of, 15)
        return one_hot((iota((rows, slots), 0) == target_row) & (lax.bitwise_and(slot_of, 15) < 11))

    gather_up_z.wait()
    up_x[x] = dot(pack(48, 64), up_z[...].reshape(64, 768)).astype(BF16)
    gather_up_x = Exchange(links, "x", lambda place: up_x.at[x], up_x)
    pair_rows = (links.row(), links.row())

    def frame_chunk(place, chunk):
        return frames_all.at[place, 128 * chunk : 128 * chunk + 128, :]

    def send_frames(chunk):
        links.send(frame_chunk(m, chunk), frame_chunk(m, chunk), pair_rows[0], chunk, chunk, pair_id)

    def take_frames(chunk):
        block = frame_chunk(pair_mate, chunk)
        links.arrive(block, pair_rows[0], chunk, pair_id)
        links.send(block, block, pair_rows[1], chunk, chunk, chip_id)

    send_frames(0)

    gather_down_y.wait()
    gather_text_first = Exchange(links, "y", lambda place: text_first.at[y], text_first)
    down_x[x, z] = dot(pack(96, 128), down_y[...].reshape(128, 768)).astype(BF16)
    above_id, above = peer_at("z", 1)
    below_id, below = peer_at("z", NZ - 1)
    from_below, from_above, from_far = links.row(), links.row(), links.row()
    from_left, from_right, from_across = links.row(), links.row(), links.row()

    def piece(column, k):
        place = (z + (0, 1, 3, 2)[k // 2]) % NZ
        return down_x.at[column, place, 48 * (k % 2) : 48 * (k % 2) + 48, :]

    def pass_down(k):
        for part in (2 * k, 2 * k + 1):
            links.send(piece(x, part), piece(x, part), from_left, part, part, right_id)
            links.send(piece(x, part), piece(x, part), from_right, part, part, left_id)

    def take_down(k):
        first, second = piece(x, 2 * k), piece(x, 2 * k + 1)
        row = (None, from_above, from_below, from_far)[k]
        links.arrive(first, row, 0, above_id)
        links.arrive(second, row, 1, above_id)
        if k == 1:
            links.send(second, second, from_far, 1, 1, below_id)
        if k == 2:
            links.send(first, first, from_far, 0, 0, above_id)
        pass_down(k)

    def take_side(k):
        links.arrive(piece(left, k), from_left, k, left_id)
        if k % 2 == 0:
            links.send(piece(left, k), piece(left, k), from_across, k, k, right_id)
        links.arrive(piece(right, k), from_right, k, right_id)
        if k % 2 == 1:
            links.send(piece(right, k), piece(right, k), from_across, k, k, left_id)

    for part in range(2):
        links.send(piece(x, part), piece(x, part), from_below, part, part, above_id)
        links.send(piece(x, part), piece(x, part), from_above, part, part, below_id)
    pass_down(0)
    feature = feature_at(iota((1, 1536), 1))
    for quarter in range(NM):
        order[quarter] = one_hot(iota((352, 1536), 0) + 352 * quarter == feature)
    gather_where = Exchange(links, "x", lambda place: where_x.at[x], where_x)

    slot_of = iota((176, 192), 1)
    from_x = (slot_of >= 48).astype(jnp.int32) + (slot_of >= 96).astype(jnp.int32) + (
        slot_of >= 144
    ).astype(jnp.int32)
    inside = slot_of - 48 * from_x
    from_z = (inside >= 11).astype(jnp.int32) + (inside >= 22).astype(jnp.int32) + (
        inside >= 33
    ).astype(jnp.int32)
    target_row = (from_z * 4 + from_x) * 11 + inside - 11 * from_z
    pack_x = one_hot((iota((176, 192), 0) == target_row) & (inside < 44))
    gather_up_x.wait()
    up_y[y] = dot(pack_x, up_x[...].reshape(192, 768)).astype(BF16)
    up_right, up_left = (links.row(), links.row()), (links.row(), links.row())

    def pass_up(step, part):
        rows = slice(0, 96) if part == 0 else slice(96, 176)
        if step < 4 or part == 0:
            ahead = up_y.at[(y - (step - 1) + NY) % NY, rows, :]
            links.send(ahead, ahead, up_right[part], step, step, up_id)
        if step < 4 or part == 1:
            behind = up_y.at[(y + (step - 1)) % NY, rows, :]
            links.send(behind, behind, up_left[part], step, step, down_id)

    def take_up(step, part):
        rows = slice(0, 96) if part == 0 else slice(96, 176)
        if step < 4 or part == 0:
            links.arrive(up_y.at[(y - step + NY) % NY, rows, :], up_right[part], step, up_id)
        if step < 4 or part == 1:
            links.arrive(up_y.at[(y + step) % NY, rows, :], up_left[part], step, down_id)
        if step < 4:
            pass_up(step + 1, part)

    pass_up(1, 0)
    pass_up(1, 1)
    gather_text_first.wait()
    for slot in range(NY):
        text_rows[4 * slot : 4 * slot + 4, :] = text_first[slot]
    text_z[z] = text_rows[...].astype(BF16)
    def normalise(step, carry):
        rows = pl.ds(pl.multiple_of(step * 32, 32), 32)
        values = [frames_all[quarter, rows, :].astype(F32) for quarter in range(NM)]
        total = sum(jnp.sum(v, axis=-1, keepdims=True) for v in values)
        squares = sum(jnp.sum(v * v, axis=-1, keepdims=True) for v in values)
        mean = total * F32(1.0 / D)
        factor = lax.rsqrt(squares * F32(1.0 / D) - mean * mean + epsilon)
        for quarter in range(NM):
            normed[quarter, rows, :] = (
                (values[quarter] - mean) * factor * norm_rows[0:1, 352 * quarter : 352 * quarter + 352]
                + norm_rows[1:2, 352 * quarter : 352 * quarter + 352]
            ).astype(BF16)
        return carry

    def normalise_chunk(chunk):
        links.arrive(frame_chunk(far_mate, chunk), pair_rows[1], chunk, chip_id)
        lax.fori_loop(4 * chunk, 4 * chunk + 4, normalise, 0)

    take_side(0)
    take_side(1)
    take_up(1, 0)
    take_down(1)
    take_down(2)
    send_frames(1)
    send_frames(2)
    send_frames(3)
    take_up(1, 1)
    take_side(2)
    take_side(3)
    take_frames(0)
    links.arrive(frames_all.at[chip_mate], frames_row, 0, chip_id)
    take_up(2, 0)
    take_side(4)
    take_frames(1)
    normalise_chunk(0)
    take_up(2, 1)
    take_side(5)
    take_down(3)
    take_frames(2)
    take_frames(3)
    gather_text_z = Exchange(links, "z", lambda place: text_z.at[z], text_z)
    normalise_chunk(1)
    take_up(3, 0)
    take_side(6)
    normalise_chunk(2)
    take_up(3, 1)
    take_side(7)
    normalise_chunk(3)

    def rows_of(place):
        return pl.ds(pl.multiple_of(place * 128, 128), 128)

    own = jnp.zeros((128, 1536), F32)
    own_bias = jnp.zeros((16, 1536), F32)
    for quarter in range(NM):
        own += dot(frames_all[quarter, rows_of(m), :], order[quarter])
        bias_part = norm_rows[2:3, 352 * quarter : 352 * quarter + 352]
        bias_rows[...] = jnp.zeros((16, 352), F32)
        for digit in range(3):
            rounded = bias_part.astype(BF16).astype(F32)
            bias_rows[digit : digit + 1, :] = rounded
            bias_part = bias_part - rounded
        own_bias += dot(bias_rows[...].astype(BF16), order[quarter])
    own = own + jnp.sum(own_bias, axis=0, keepdims=True)
    for block in range(NX):
        resid[block] = own[:, 384 * block : 384 * block + 384]
    turn = one_hot(iota((1536, 352), 1) + 352 * m == feature_at(iota((1536, 1), 0)))
    projection_rows[...] = dot(turn, projection_ref[...]).astype(BF16)
    bias_rows[...] = jnp.zeros((16, 352), F32)
    for row, vector in enumerate((final_gain_ref, final_bias_ref)):
        rest = vector[...].reshape(1, 352)
        for part in range(3):
            rounded = rest.astype(BF16).astype(F32)
            bias_rows[3 * row + part : 3 * row + part + 1, :] = rounded
            rest = rest - rounded
    final_parts = dot(bias_rows[...].astype(BF16), order[m])
    final_rows[0:1, :] = jnp.sum(final_parts[0:3, :], axis=0, keepdims=True)
    final_rows[1:2, :] = jnp.sum(final_parts[3:6, :], axis=0, keepdims=True)
    take_up(4, 0)
    take_up(4, 1)
    arrival = [x, left, right, across]

    def hidden_of(side):
        rows = pl.ds(pl.multiple_of(side * 256, 256), 256)
        total = jnp.broadcast_to(up_bias_ref[...].reshape(1, 768), (256, 768))
        for quarter in range(NM):
            total += dot(
                normed[quarter, rows, :],
                up_y[2 * quarter : 2 * quarter + 2].reshape(352, 768),
            )
        hidden[...] = gelu(total).astype(BF16)

    def partial_sums(block):
        sums = dot_t(hidden[...], down_x[block].reshape(384, 768))
        partial[0] = sums[0:128]
        partial[1] = sums[128:256]

    chip_rows, pair_row = (links.row(), links.row()), links.row()

    def pass_pair(k):
        links.arrive(chip_in.at[0, k], chip_rows[0], k, chip_id)
        pair_out[k] = (waiting[k] + chip_in[0, k].astype(F32)).astype(BF16)
        links.send(pair_out.at[k], pair_in.at[k], pair_row, k, k, pair_id)

    hidden_of(1 - half)
    for k, block in enumerate(arrival):
        if k == 3:
            for part in range(2 * NZ):
                links.arrive(piece(across, part), from_across, part, right_id)
        partial_sums(block)
        chip_out[0, k] = partial[1 - core].astype(BF16)
        links.send(chip_out.at[0, k], chip_in.at[0, k], chip_rows[0], k, k, chip_id)
        waiting[k] = partial[core]
        if k > 0:
            pass_pair(k - 1)
    pass_pair(3)
    hidden_of(half)
    for k, block in enumerate(arrival):
        partial_sums(block)
        chip_out[1, k] = partial[1 - core].astype(BF16)
        links.send(chip_out.at[1, k], chip_in.at[1, k], chip_rows[1], k, k, chip_id)
        resid[block] += partial[core]
    for k, block in enumerate(arrival):
        links.arrive(chip_in.at[1, k], chip_rows[1], k, chip_id)
        resid[block] += chip_in[1, k].astype(F32)
    gather_text_z.wait()
    gather_where.wait()
    total, squares = jnp.zeros((128, 1), F32), jnp.zeros((128, 1), F32)
    for k, block in enumerate(arrival):
        links.arrive(pair_in.at[k], pair_row, k, pair_id)
        values = resid[block] + pair_in[k].astype(F32)
        resid[block] = values
        total += jnp.sum(values, axis=-1, keepdims=True)
        squares += jnp.sum(values * values, axis=-1, keepdims=True)
    means = total * F32(1.0 / D)
    factors = lax.rsqrt(squares * F32(1.0 / D) - means * means + epsilon)

    for clip in range(4):
        rows = slice(32 * clip, 32 * clip + 32)
        values = [resid[block, rows, :] for block in range(NX)]
        mean, factor = means[rows], factors[rows]
        count = jnp.full((32, 1), counts_ref[m * 4 + clip], jnp.int32)
        weight = jnp.where(iota((32, 1), 0) < count, factor / count.astype(F32), F32(0.0))
        for block in range(NX):
            lanes = slice(384 * block, 384 * block + 384)
            pool_in[m, clip : clip + 1, lanes] = jnp.sum(
                (values[block] - mean) * weight, axis=0, keepdims=True
            )
    share_pool = Exchange(links, "m", lambda place: pool_in.at[m], pool_in)
    share_pool.wait()
    for slot in range(NM):
        pool_all[4 * slot : 4 * slot + 4, :] = pool_in[slot]
    pooled = (pool_all[...] * final_rows[0:1, :] + final_rows[1:2, :]).astype(BF16)
    raw_in[m] = dot(pooled, projection_rows[...]).astype(BF16)
    share_raw = Exchange(links, "m", lambda place: raw_in.at[m], raw_in)
    share_raw.wait()
    raw = raw_in[0].astype(F32)
    for slot in range(1, NM):
        raw += raw_in[slot].astype(F32)

    embed = raw * lax.rsqrt(jnp.sum(raw * raw, axis=-1, keepdims=True) + epsilon)
    embed_ref[...] = embed
    video_x[x] = embed.astype(BF16)
    gather_video = Exchange(links, "x", lambda place: video_x.at[x], video_x)
    column = iota((NX * 16, NY * 16), 1)
    owner = lax.bitwise_and(lax.shift_right_logical(column, 2), 7) * NZ + lax.shift_right_logical(column, 5)
    ids = (((owner * 4) + x) * 4 + m) * 4 + lax.bitwise_and(column, 3)
    labels = jnp.where(ids == where_x[...].reshape(NX * 16, 128), F32(1.0), F32(-1.0))
    text = text_z[...].reshape(NY * 16, E)
    row_of = iota((128, 128), 0)
    moved = (
        lax.bitwise_and(lax.shift_right_logical(row_of, 2), 3) * 32
        + lax.shift_right_logical(row_of, 4) * 4
        + lax.bitwise_and(row_of, 3)
    )
    reorder = one_hot(iota((128, 128), 1) == moved)
    gather_video.wait()
    video = video_x[...].reshape(NX * 16, E)
    logits = scale * dot_t(video, text) + bias
    pair_weights = -labels * lax.logistic(-labels * logits)
    turned = jnp.transpose(pair_weights).astype(BF16)
    by_y = dot(reorder, turned).astype(BF16)
    text_out_y[...] = (scale * dot(by_y, video[:, 0:512])).astype(BF16).reshape(NY, 16, 512)
    text_in_y[y] = text_out_y[y]
    reduce_first_y = Exchange(links, "y", lambda place: text_out_y.at[place], text_in_y)
    text_out_z[...] = (scale * dot(turned, video[:, 512:1024])).astype(BF16).reshape(NZ, 32, 512)
    text_in_z[z] = text_out_z[z]
    reduce_first_z = Exchange(links, "z", lambda place: text_out_z.at[place], text_in_z)
    video_out[...] = (scale * dot(pair_weights.astype(BF16), text)).astype(BF16).reshape(NX, 16, E)
    video_in[x] = video_out[x]
    reduce_video_x = Exchange(links, "x", lambda place: video_out.at[place], video_in)

    reduce_video_x.wait()
    video_total = video_in[0].astype(F32)
    for slot in range(1, NX):
        video_total += video_in[slot].astype(F32)
    mp_in[m] = video_total.astype(BF16)
    share_video = Exchange(links, "m", lambda place: mp_in.at[m], mp_in)
    reduce_first_z.wait()
    text_total = text_in_z[0].astype(F32)
    for slot in range(1, NZ):
        text_total += text_in_z[slot].astype(F32)
    text_sum_z[...] = text_total
    for slot in range(NY):
        text_part_y[slot] = text_sum_z[4 * slot : 4 * slot + 4, :]
    text_last_y[y] = text_part_y[y]
    reduce_last_y = Exchange(links, "y", lambda place: text_part_y.at[place], text_last_y)
    reduce_first_y.wait()
    text_total = text_in_y[0].astype(F32)
    for slot in range(1, NY):
        text_total += text_in_y[slot].astype(F32)
    text_sum_y[...] = text_total
    for slot in range(NZ):
        text_part_z[slot] = text_sum_y[4 * slot : 4 * slot + 4, :]
    text_last_z[z] = text_part_z[z]
    reduce_last_z = Exchange(links, "z", lambda place: text_part_z.at[place], text_last_z)
    share_video.wait()
    video_grad = mp_in[0].astype(F32)
    for slot in range(1, NM):
        video_grad += mp_in[slot].astype(F32)
    video_ref[...] = video_grad
    reduce_last_y.wait()
    text_grad = text_last_y[0]
    for slot in range(1, NY):
        text_grad += text_last_y[slot]
    text_ref[:, 512:1024] = text_grad
    reduce_last_z.wait()
    text_grad = text_last_z[0]
    for slot in range(1, NZ):
        text_grad += text_last_z[slot]
    text_ref[:, 0:512] = text_grad
    links.finish()


def on_device(
    frames,
    frame_counts,
    norm_gain,
    norm_bias,
    up_weight,
    up_bias,
    down_weight,
    down_bias,
    final_gain,
    final_bias,
    projection,
    captions,
    positives,
    logit_scale,
    logit_bias,
):
    vmem = pl.BlockSpec(memory_space=pltpu.VMEM)
    hbm = pl.BlockSpec(memory_space=pltpu.HBM)
    return pl.pallas_call(
        step_kernel,
        out_shape=(
            jax.ShapeDtypeStruct((16, E), F32),
            jax.ShapeDtypeStruct((16, E), F32),
            jax.ShapeDtypeStruct((4, E), F32),
        ),
        in_specs=[hbm] * 15,
        out_specs=(vmem, vmem, vmem),
        scratch_shapes=[
            pltpu.SMEM((16,), jnp.int32),
            pltpu.VMEM((D,), F32),
            pltpu.VMEM((D,), F32),
            pltpu.VMEM((11, 768), BF16),
            pltpu.VMEM((768,), F32),
            pltpu.VMEM((11, 768), BF16),
            pltpu.VMEM((D,), F32),
            pltpu.VMEM((352,), F32),
            pltpu.VMEM((352,), F32),
            pltpu.VMEM((352, E), BF16),
            pltpu.VMEM((4, E), BF16),
            pltpu.SMEM((16,), jnp.int32),
            pltpu.SMEM((1,), F32),
            pltpu.SMEM((1,), F32),
            pltpu.VMEM((8, D), F32),
            pltpu.VMEM((NZ, 16, 768), BF16),
            pltpu.VMEM((NY, 16, 768), BF16),
            pltpu.VMEM((1536, E), BF16),
            pltpu.VMEM((8, 1536), F32),
            pltpu.VMEM((256, 768), BF16),
            pltpu.VMEM((2, 128, 384), F32),
            pltpu.VMEM((NX, 128, 384), F32),
            pltpu.VMEM((NX, 48, 768), BF16),
            pltpu.VMEM((NY, 176, 768), BF16),
            pltpu.VMEM((NX, NZ, 96, 768), BF16),
            pltpu.VMEM((NM, 512, 352), BF16),
            pltpu.VMEM((NM, 512, 352), BF16),
            pltpu.VMEM((NM, 352, 1536), BF16),
            pltpu.VMEM((16, 352), F32),
            pltpu.VMEM((NX, 128, 384), F32),
            pltpu.VMEM((2, NX, 128, 384), BF16),
            pltpu.VMEM((2, NX, 128, 384), BF16),
            pltpu.VMEM((NX, 128, 384), BF16),
            pltpu.VMEM((NX, 128, 384), BF16),
            pltpu.VMEM((NM, 4, 1536), F32),
            pltpu.VMEM((16, 1536), F32),
            pltpu.VMEM((NM, 16, E), BF16),
            pltpu.VMEM((NY, 4, E), F32),
            pltpu.VMEM((32, E), F32),
            pltpu.VMEM((NZ, 32, E), BF16),
            pltpu.VMEM((NX, 16, E), BF16),
            pltpu.VMEM((NX, 16, 128), jnp.int32),
            pltpu.VMEM((NY, 16, 512), BF16),
            pltpu.VMEM((NY, 16, 512), BF16),
            pltpu.VMEM((NZ, 32, 512), BF16),
            pltpu.VMEM((NZ, 32, 512), BF16),
            pltpu.VMEM((NX, 16, E), BF16),
            pltpu.VMEM((NX, 16, E), BF16),
            pltpu.VMEM((16, 512), F32),
            pltpu.VMEM((32, 512), F32),
            pltpu.VMEM((NY, 4, 512), F32),
            pltpu.VMEM((NZ, 4, 512), F32),
            pltpu.VMEM((NY, 4, 512), F32),
            pltpu.VMEM((NZ, 4, 512), F32),
            pltpu.VMEM((NM, 16, E), BF16),
            pltpu.SemaphoreType.DMA((36, 8)),
            pltpu.SemaphoreType.DMA((36, 8)),
            pltpu.SemaphoreType.DMA((15,)),
        ],
        compiler_params=pltpu.CompilerParams(
            collective_id=0, has_side_effects=True, vmem_limit_bytes=56 * 1024 * 1024
        ),
    )(
        frames.reshape(512, 352),
        frame_counts,
        norm_gain,
        norm_bias,
        up_weight,
        up_bias,
        down_weight,
        down_bias,
        final_gain,
        final_bias,
        projection,
        captions,
        positives,
        logit_scale.reshape(1),
        logit_bias.reshape(1),
    )


def solution(mesh):
    return jax.shard_map(
        on_device,
        mesh=mesh,
        in_specs=(
            P("dp", None, "mp"),
            P("dp"),
            P(),
            P(),
            P("dp", "mp"),
            P("mp"),
            P("dp", "mp"),
            P(),
            P("mp"),
            P("mp"),
            P("mp", None),
            P(("dp", "mp"), None),
            P("dp"),
            P(),
            P(),
        ),
        out_specs=(P("dp", None), P("dp", None), P(("dp", "mp"), None)),
        check_vma=False,
    )
```
